512 devices in a mesh: draw: 16 (over y_hi, x, core), blk: 32 (over y_lo, z).
Axes of the slice: x: 4, y: 4 (y_hi: 2, y_lo: 2; y = y_hi * 2 + y_lo), z: 16, core: 2. Of those that a mesh axis runs over, the one named last changes fastest.
Arguments:
- field: bfloat16 [12288, 4096], P('draw', 'blk'), may hold values from -8 to 8
- backward: bfloat16 [12288, 4096], P('draw', 'blk'), may hold values from -6 to 6
Outputs:
- feature_kernel: float32 [4096, 4096], P('blk', 'draw')
- gradient_kernel: float32 [4096, 4096], P('blk', 'draw')
The draws below stay inside these ranges and needn't reach their ends.
All inputs are finite; a program needn't handle non-finite values.
Results may differ from the reference program's by a relative error of at most 0.002.
Values may be sent and summed in bfloat16 or wider, within the bound.
No kernel may reach another device: no remote copies, remote signals or barrier semaphores. Data moves between devices by JAX's collectives and lax.ppermute only.
A program may use at most 64 MiB of HBM per device.

```python
import jax
import jax.numpy as jnp

DRAWS = 12288
COLS = 4096


def block_levels(key, extent, pieces, least, largest):
    level = 1.0
    for dim, blocks in pieces:
        draws = jax.random.uniform(jax.random.fold_in(jax.random.fold_in(key, 6), dim), (blocks,), jnp.float32, least / len(pieces), largest / len(pieces))
        level = level * jnp.repeat(jnp.exp(draws), extent[dim] // blocks).reshape((-1,) + (1,) * (len(extent) - 1 - dim))
    return level


def normal_values(rng, shape, width, limit, split=(), dtype=jnp.bfloat16):
    factor_of = block_levels(rng, shape, split, -0.22, 0.18) if split else 1.0
    drawn = jax.random.normal(rng, shape, jnp.float32) * width * factor_of
    return jnp.minimum(jnp.maximum(drawn, -limit), limit).astype(dtype)


def setup_inputs(seed: int = 0) -> dict:
    arg_keys = jax.random.split(jax.random.key(seed), 3)
    field = normal_values(arg_keys[0], (DRAWS, COLS), 1.5, 8.0, ((0, 16), (1, 32)))
    backward = normal_values(arg_keys[1], (DRAWS, COLS), 1.0, 6.0, ((0, 16), (1, 32)))
    return {"field": field, "backward": backward}


def reference(field, backward):
    wide = jnp.tanh(field.astype(jnp.float32))
    activity = wide.astype(jnp.bfloat16)
    signal = ((1.0 - wide * wide) * backward.astype(jnp.float32)).astype(jnp.bfloat16)
    feature_kernel = jnp.dot(activity.T, activity, preferred_element_type=jnp.float32) / DRAWS
    gradient_kernel = jnp.dot(signal.T, signal, preferred_element_type=jnp.float32) / DRAWS
    return feature_kernel, gradient_kernel
```

```python
import functools

import jax
import jax.numpy as jnp
import numpy as np
from jax import lax
from jax.experimental import pallas as pl
from jax.experimental.pallas import tpu as pltpu
from jax.sharding import Mesh, PartitionSpec as P

AXES = ("yh", "x", "c", "yl", "z")
SIZES = (2, 4, 2, 2, 16)
EXTRA = 16
VMEM = pl.BlockSpec(memory_space=pltpu.VMEM)
SMEM = pl.BlockSpec(memory_space=pltpu.SMEM)
PARAMS = pltpu.CompilerParams(vmem_limit_bytes=40 * 1024 * 1024)


def device_index(yh, x, c, yl, z):
    return (((yh * 4 + x) * 2 + c) * 2 + yl) * 16 + z


def home(row_y, row_z, col_y, col_z):
    return device_index(col_y, col_z // 4, col_z % 4 // 2, row_y, row_z), col_z % 2


def homes(yh, x, c, yl, z):
    top, bottom = yl, yh
    if c == 0:
        left, right = [(z + 4, z - 1), (z + 4, z - 2), (z, z - 3), (z, z - 4)][x]
    elif x < 3:
        left, right = [(z, z + 1), (z, z + 2), (z - 4, z + 3)][x]
    elif yl == 0:
        left, right = z - 4, z + 4
        if yh == 0:
            top = bottom = 0 if z < 8 else 1
    elif yh == 1:
        return [home(0, z, 0, z) + (2,), home(1, z, 1, z) + (3,)]
    else:
        left = right = z
        top, bottom = 0, 1
    left, right = left % 16, right % 16
    return [home(top, left, bottom, right) + (0,), home(bottom, right, top, left) + (1,)]


def routes():
    edges = []
    for place in np.ndindex(*SIZES):
        for to, half, mode in homes(*place):
            edges.append((device_index(*place), to, half, mode))
    into = [[] for _ in range(512)]
    for e, edge in enumerate(edges):
        into[edge[1]].append(e)
    turn = [-1] * len(edges)
    for first in range(len(edges)):
        e = first
        while turn[e] < 0:
            turn[e] = 0
            pair = into[edges[e][1]]
            other = pair[0] + pair[1] - e
            turn[other] = 1
            e = other ^ 1
    perms = [[], []]
    table = np.zeros((512, 4), np.int32)
    for e, (source, to, half, mode) in enumerate(edges):
        perms[turn[e]].append((source, to))
        table[to, 2 * half] = turn[e]
        table[to, 2 * half + 1] = mode
    return perms, table


def features_kernel(place, field, backward, keep, send):
    rows = field.shape[0] // 2
    mine = place[1]
    for out, half in ((keep, mine), (send, 1 - mine)):
        part = pl.ds(pl.multiple_of(half * rows, rows), rows)
        wide = jnp.tanh(field[part, :].astype(jnp.float32))
        out[0] = wide.astype(jnp.bfloat16)
        out[1] = ((1.0 - wide * wide) * backward[part, :].astype(jnp.float32)).astype(
            jnp.bfloat16
        )


def products_kernel(place, *refs):
    walk, far, out, scratch = refs[:10], refs[10:12], refs[12], refs[13]
    core, y, z = place[0], place[1], place[2]
    n = out.shape[-1]
    w = [(walk[2 * j], walk[2 * j + 1]) for j in range(5)]

    def product(left, right, kernel):
        total = None
        for c in range(2):
            lhs = jnp.concatenate([left[0][c, kernel], left[1][c, kernel]], axis=1)
            rhs = jnp.concatenate([right[0][c, kernel], right[1][c, kernel]], axis=1)
            term = lax.dot_general(
                lhs, rhs, (((0,), (0,)), ((), ())), preferred_element_type=jnp.float32
            )
            total = term if total is None else total + term
        return total

    def store(x, kernel, total):
        for p in range(2):
            for q in range(2):
                out[q ^ y, x, p ^ y, kernel, 0:n] = total[
                    p * n : (p + 1) * n, q * n : (q + 1) * n
                ].astype(jnp.bfloat16)

    def keep(at, total):
        for p in range(2):
            for q in range(2):
                scratch[at, p ^ y, q ^ y] = total[
                    p * n : (p + 1) * n, q * n : (q + 1) * n
                ]

    for yh in range(2):
        for x in range(4):
            for yl in range(2):
                for kernel in range(2):
                    out[yh, x, yl, kernel, n : n + EXTRA] = jnp.zeros(
                        (EXTRA, n), jnp.bfloat16
                    )

    @pl.when(core == 0)
    def _():
        for kernel in range(2):
            store(0, kernel, product(far, w[1], kernel))
            store(1, kernel, product(far, w[2], kernel))
            store(2, kernel, product(w[0], w[3], kernel))
            store(3, kernel, product(w[0], w[4], kernel))

    @pl.when(core == 1)
    def _():
        row = lax.broadcasted_iota(jnp.int32, (n, n), 0)
        col = lax.broadcasted_iota(jnp.int32, (n, n), 1)
        for kernel in range(2):
            store(0, kernel, product(w[0], w[1], kernel))
            store(1, kernel, product(w[0], w[2], kernel))
            store(2, kernel, product(far, w[3], kernel))
            keep(0, product(far, w[4], kernel))
            keep(1, product(w[0], w[0], kernel))
            side = jnp.where(z < 8, 0, 1)
            out[1, 3, 0, kernel, 0:n] = scratch[0, 0, 1].astype(jnp.bfloat16)
            out[0, 3, 0, kernel, 0:n] = scratch[0, side, side].astype(jnp.bfloat16)
            out[0, 3, 1, kernel, 0:n] = scratch[1, 0, 1].astype(jnp.bfloat16)
            low = scratch[1, 1, 1]
            out[1, 3, 1, kernel, 0:n] = jnp.where(
                row <= col, scratch[1, 0, 0], low
            ).astype(jnp.bfloat16)
            diagonal = jnp.sum(jnp.where(row == col, low, 0.0), axis=0, keepdims=True)
            out[1, 3, 1, kernel, n : n + EXTRA] = jnp.broadcast_to(
                diagonal, (EXTRA, n)
            ).astype(jnp.bfloat16)


def place_kernel(total_draws, todo, a, b, feature, gradient):
    n = feature.shape[0]
    row = lax.broadcasted_iota(jnp.int32, (n, n), 0)
    col = lax.broadcasted_iota(jnp.int32, (n, n), 1)
    for kernel, out in enumerate((feature, gradient)):
        for half in range(2):
            second, mode = todo[2 * half] == 1, todo[2 * half + 1]
            got = jnp.where(second, b[kernel, 0:n], a[kernel, 0:n])
            extra = jnp.where(second, b[kernel, n : n + 1], a[kernel, n : n + 1])
            turned = got.T
            lower = row > col
            plain = (mode == 0) | ((mode == 2) & (row <= col)) | ((mode == 3) & lower)
            value = jnp.where(plain, got, turned)
            value = jnp.where((mode == 3) & (row == col), extra, value)
            out[:, half * n : (half + 1) * n] = value / total_draws


def on_device(field, backward):
    draws, n = field.shape
    total_draws = draws * 16
    place = jnp.stack([lax.axis_index("c"), lax.axis_index("yl"), lax.axis_index("z")])
    half = jax.ShapeDtypeStruct((2, draws // 2, n), jnp.bfloat16)
    keep, send = pl.pallas_call(
        features_kernel,
        out_shape=(half, half),
        in_specs=[SMEM, VMEM, VMEM],
        out_specs=(VMEM, VMEM),
        compiler_params=PARAMS,
    )(place, field, backward)

    swap = [(0, 1), (1, 0)]
    other = lax.ppermute(send, "yl", swap)
    chains = [lax.all_gather(keep, "c"), lax.all_gather(other, "c")]
    step = [
        (c * 16 + z, c * 16 + (z + 1 - 2 * c) % 16) for c in range(2) for z in range(16)
    ]
    walk = list(chains)
    for _ in range(4):
        chains = [lax.ppermute(chain, ("c", "z"), step) for chain in chains]
        walk += chains
    far = [lax.ppermute(chain, "c", swap) for chain in chains]

    partial = pl.pallas_call(
        products_kernel,
        out_shape=jax.ShapeDtypeStruct((2, 4, 2, 2, n + EXTRA, n), jnp.bfloat16),
        in_specs=[SMEM] + [VMEM] * 12,
        out_specs=VMEM,
        scratch_shapes=[pltpu.VMEM((2, 2, 2, n, n), jnp.float32)],
        compiler_params=PARAMS,
    )(place, *walk, *far)
    partial = partial.reshape(16, 2, n + EXTRA, n)
    partial = lax.all_to_all(partial, ("yh", "x", "yl"), 0, 0, tiled=True)
    block = jnp.sum(partial.astype(jnp.float32), axis=0)

    perms, table = routes()
    a = lax.ppermute(block, AXES, perms[0])
    b = lax.ppermute(block, AXES, perms[1])
    todo = lax.dynamic_index_in_dim(
        jnp.asarray(table), lax.axis_index(AXES), 0, keepdims=False
    )
    out = jax.ShapeDtypeStruct((n, 2 * n), jnp.float32)
    return pl.pallas_call(
        functools.partial(place_kernel, total_draws),
        out_shape=(out, out),
        in_specs=[SMEM, VMEM, VMEM],
        out_specs=(VMEM, VMEM),
        compiler_params=PARAMS,
    )(todo, a, b)


def solution(mesh):
    grid = Mesh(mesh.devices.reshape(SIZES), AXES)
    return jax.shard_map(
        on_device,
        mesh=grid,
        in_specs=(P(("yh", "x", "c"), ("yl", "z")),) * 2,
        out_specs=(P(("yl", "z"), ("yh", "x", "c")),) * 2,
        check_vma=False,
    )
```

```python
import functools

import jax
import jax.numpy as jnp
import numpy as np
from jax import lax
from jax.experimental import pallas as pl
from jax.experimental.pallas import tpu as pltpu
from jax.sharding import Mesh, PartitionSpec as P

AXES = ("yh", "x", "c", "yl", "z")
SIZES = (2, 4, 2, 2, 16)
EXTRA = 16
VMEM = pl.BlockSpec(memory_space=pltpu.VMEM)
SMEM = pl.BlockSpec(memory_space=pltpu.SMEM)
PARAMS = pltpu.CompilerParams(vmem_limit_bytes=40 * 1024 * 1024)


def device_index(yh, x, c, yl, z):
    return (((yh * 4 + x) * 2 + c) * 2 + yl) * 16 + z


def home(row_y, row_z, col_y, col_z):
    return device_index(col_y, col_z // 4, col_z % 4 // 2, row_y, row_z), col_z % 2


def homes(yh, x, c, yl, z):
    slot = yh * 4 + x
    if c == 0:
        left, right = (1 - yl, z if slot > 3 else z + 4), (yl, z - slot % 4 - 1)
        if slot == 3 and yl == 1:
            left, right = (0, z), (1, z)
    else:
        left, right = (yl, z if slot > 3 else z - 4), (yl, z + slot % 4 + 1)
        if slot == 3 and (z < 8) != (yl == 0):
            return [home(0, z, 0, z) + (2,), home(1, z, 1, z) + (3,)]
    left, right = (left[0], left[1] % 16), (right[0], right[1] % 16)
    return [home(*left, *right) + (0,), home(*right, *left) + (1,)]


def routes():
    edges = []
    for place in np.ndindex(*SIZES):
        for to, half, mode in homes(*place):
            edges.append((device_index(*place), to, half, mode))
    into = [[] for _ in range(512)]
    for e, edge in enumerate(edges):
        into[edge[1]].append(e)
    turn = [-1] * len(edges)
    for first in range(len(edges)):
        e = first
        while turn[e] < 0:
            turn[e] = 0
            pair = into[edges[e][1]]
            other = pair[0] + pair[1] - e
            turn[other] = 1
            e = other ^ 1
    perms = [[], []]
    table = np.zeros((512, 4), np.int32)
    for e, (source, to, half, mode) in enumerate(edges):
        perms[turn[e]].append((source, to))
        table[to, 2 * half] = turn[e]
        table[to, 2 * half + 1] = mode
    return perms, table


def features_kernel(field, backward, activity, signal, f, b, sems):
    copies = [
        pltpu.make_async_copy(field, f, sems.at[0]),
        pltpu.make_async_copy(backward, b, sems.at[1]),
    ]
    for copy in copies:
        copy.start()
    for copy in copies:
        copy.wait()
    wide = jnp.tanh(f[...].astype(jnp.float32))
    activity[...] = wide.astype(jnp.bfloat16)
    signal[...] = ((1.0 - wide * wide) * b[...].astype(jnp.float32)).astype(
        jnp.bfloat16
    )


def products_kernel(place, scale, *refs):
    out = refs[-1]
    core, y, z = place[0], place[1], place[2]
    n = out.shape[-1]
    row = lax.broadcasted_iota(jnp.int32, (n, n), 0)
    col = lax.broadcasted_iota(jnp.int32, (n, n), 1)

    def product(left, right):
        return lax.dot_general(
            left, right, (((0,), (0,)), ((), ())), preferred_element_type=jnp.float32
        )

    def store(slot, kernel, total):
        out[slot, kernel * n : (kernel + 1) * n] = (total * scale[0]).astype(
            jnp.bfloat16
        )

    for slot in range(8):
        out[slot, 2 * n : 2 * n + EXTRA] = jnp.zeros((EXTRA, n), jnp.bfloat16)
    packed = (core == 1) & ((z < 8) != (y == 0))
    for kernel in range(2):
        walk, near, far = refs[kernel : 10 + kernel : 2], refs[10 + kernel], refs[12 + kernel]
        steps = jnp.concatenate([w[...] for w in walk[1:]], axis=1)

        def four(first, left):
            total = product(left, steps)
            for j in range(4):
                store(first + j, kernel, total[:, j * n : (j + 1) * n])

        four(0, far[...])

        @pl.when(core == 0)
        def _():
            four(4, near[...])

        @pl.when(core == 1)
        def _():
            four(4, walk[0][...])

        @pl.when((core == 0) & (y == 1))
        def _():
            store(3, kernel, product(near[...], walk[0][...]))

        @pl.when(packed)
        def _():
            own = product(walk[0][...], walk[0][...])
            other = product(near[...], near[...])
            high = jnp.where(y == 0, own, other)
            low = jnp.where(y == 0, other, own)
            store(3, kernel, jnp.where(row <= col, high, low))
            diagonal = jnp.sum(jnp.where(row == col, low, 0.0), axis=0, keepdims=True)
            line = lax.broadcasted_iota(jnp.int32, (EXTRA, n), 0)
            extra = out[3, 2 * n : 2 * n + EXTRA].astype(jnp.float32)
            extra = jnp.where(line == kernel, diagonal * scale[0], extra)
            out[3, 2 * n : 2 * n + EXTRA] = extra.astype(jnp.bfloat16)


def place_kernel(total_draws, todo, a, b, feature, gradient):
    n = feature.shape[0]
    row = lax.broadcasted_iota(jnp.int32, (n, n), 0)
    col = lax.broadcasted_iota(jnp.int32, (n, n), 1)
    for kernel, out in enumerate((feature, gradient)):
        block, line = pl.ds(kernel * n, n), pl.ds(2 * n + kernel, 1)
        for half in range(2):
            second, mode = todo[2 * half] == 1, todo[2 * half + 1]
            got = jnp.where(second, b[block, :], a[block, :])
            extra = jnp.where(second, b[line, :], a[line, :])
            turned = got.T
            lower = row > col
            plain = (mode == 0) | ((mode == 2) & (row <= col)) | ((mode == 3) & lower)
            value = jnp.where(plain, got, turned)
            value = jnp.where((mode == 3) & (row == col), extra, value)
            out[:, half * n : (half + 1) * n] = value / total_draws


def on_device(field, backward):
    draws, n = field.shape
    total_draws = draws * 16
    values = jax.ShapeDtypeStruct((draws, n), jnp.bfloat16)
    own = pl.pallas_call(
        features_kernel,
        out_shape=(values, values),
        in_specs=[pl.BlockSpec(memory_space=pl.ANY)] * 2,
        out_specs=(VMEM, VMEM),
        scratch_shapes=[
            pltpu.VMEM((draws, n), jnp.bfloat16),
            pltpu.VMEM((draws, n), jnp.bfloat16),
            pltpu.SemaphoreType.DMA((2,)),
        ],
        compiler_params=PARAMS,
    )(field, backward)

    step = [
        (c * 16 + z, c * 16 + (z + 1 - 2 * c) % 16) for c in range(2) for z in range(16)
    ]
    chains = [lax.all_gather(part, "c", axis=0, tiled=True) for part in own]
    start, walk = chains, list(chains)
    for j in range(4):
        chains = [lax.ppermute(chain, ("c", "z"), step) for chain in chains]
        walk += chains
        if j == 0:
            start = lax.optimization_barrier((start, chains))[0]
    near = [lax.ppermute(part, "yl", [(0, 1), (1, 0)]) for part in start]
    cross = [(0, 2), (1, 3), (2, 1), (3, 0)]
    far = [lax.ppermute(chain, ("c", "yl"), cross) for chain in chains]

    place = jnp.stack([lax.axis_index("c"), lax.axis_index("yl"), lax.axis_index("z")])
    scales = np.exp2(np.arange(8) / 8).astype(np.float32)
    scale = lax.dynamic_slice_in_dim(
        jnp.asarray(scales), lax.axis_index(("yh", "x")), 1
    )
    partial = pl.pallas_call(
        products_kernel,
        out_shape=jax.ShapeDtypeStruct((8, 2 * n + EXTRA, n), jnp.bfloat16),
        in_specs=[SMEM, SMEM] + [VMEM] * 14,
        out_specs=VMEM,
        compiler_params=PARAMS,
    )(place, scale, *walk, *near, *far)
    partial = lax.all_to_all(partial, ("yh", "x"), 0, 0, tiled=True)
    block = jnp.sum(partial.astype(jnp.float32) / scales[:, None, None], axis=0)
    block = block[: 2 * n + 8]

    perms, table = routes()
    a = lax.ppermute(block, AXES, perms[0])
    b = lax.ppermute(block, AXES, perms[1])
    todo = lax.dynamic_index_in_dim(
        jnp.asarray(table), lax.axis_index(AXES), 0, keepdims=False
    )
    out = jax.ShapeDtypeStruct((n, 2 * n), jnp.float32)
    return pl.pallas_call(
        functools.partial(place_kernel, total_draws),
        out_shape=(out, out),
        in_specs=[SMEM, VMEM, VMEM],
        out_specs=(VMEM, VMEM),
        compiler_params=PARAMS,
    )(todo, a, b)


def solution(mesh):
    grid = Mesh(mesh.devices.reshape(SIZES), AXES)
    return jax.shard_map(
        on_device,
        mesh=grid,
        in_specs=(P(("yh", "x", "c"), ("yl", "z")),) * 2,
        out_specs=(P(("yl", "z"), ("yh", "x", "c")),) * 2,
        check_vma=False,
    )
```

```python
import functools

import jax
import jax.numpy as jnp
import numpy as np
from jax import lax
from jax.experimental import pallas as pl
from jax.experimental.pallas import tpu as pltpu
from jax.sharding import Mesh, PartitionSpec as P

AXES = ("yh", "x", "c", "yl", "z")
SIZES = (2, 4, 2, 2, 16)
PIECES = 4
EXTRA = 16
VMEM = pl.BlockSpec(memory_space=pltpu.VMEM)
SMEM = pl.BlockSpec(memory_space=pltpu.SMEM)
PARAMS = pltpu.CompilerParams(vmem_limit_bytes=40 * 1024 * 1024)


def device_index(yh, x, c, yl, z):
    return (((yh * 4 + x) * 2 + c) * 2 + yl) * 16 + z


def home(row_y, row_z, col_y, col_z):
    return device_index(col_y, col_z // 4, col_z % 4 // 2, row_y, row_z), col_z % 2


def homes(yh, x, c, yl, z):
    slot = yh * 4 + x
    if c == 0:
        left, right = (1 - yl, z if slot > 3 else z + 4), (yl, z - slot % 4 - 1)
        if slot == 3 and yl == 1:
            left, right = (0, z), (1, z)
    else:
        left, right = (yl, z if slot > 3 else z - 4), (yl, z + slot % 4 + 1)
        if slot == 3 and (z < 8) != (yl == 0):
            return [home(0, z, 0, z) + (2,), home(1, z, 1, z) + (3,)]
    left, right = (left[0], left[1] % 16), (right[0], right[1] % 16)
    return [home(*left, *right) + (0,), home(*right, *left) + (1,)]


def routes():
    edges = []
    for place in np.ndindex(*SIZES):
        for to, half, mode in homes(*place):
            edges.append((device_index(*place), to, half, mode))
    into = [[] for _ in range(512)]
    for e, edge in enumerate(edges):
        into[edge[1]].append(e)
    turn = [-1] * len(edges)
    for first in range(len(edges)):
        e = first
        while turn[e] < 0:
            turn[e] = 0
            pair = into[edges[e][1]]
            other = pair[0] + pair[1] - e
            turn[other] = 1
            e = other ^ 1
    perms = [[], []]
    table = np.zeros((512, 4), np.int32)
    for e, (source, to, half, mode) in enumerate(edges):
        perms[turn[e]].append((source, to))
        table[to, 2 * half] = turn[e]
        table[to, 2 * half + 1] = mode
    return perms, table


def features_kernel(field, backward, activity, signal, f, b, sems):
    rows = field.shape[0] // PIECES
    copies = []
    for piece in range(PIECES):
        part = pl.ds(piece * rows, rows)
        copies.append(
            [
                pltpu.make_async_copy(src.at[part], dst.at[part], sems.at[i, piece])
                for i, (src, dst) in enumerate(((field, f), (backward, b)))
            ]
        )
        for copy in copies[-1]:
            copy.start()
    for piece in range(PIECES):
        part = pl.ds(piece * rows, rows)
        for copy in copies[piece]:
            copy.wait()
        wide = jnp.tanh(f[part, :].astype(jnp.float32))
        activity[part, :] = wide.astype(jnp.bfloat16)
        signal[part, :] = (
            (1.0 - wide * wide) * b[part, :].astype(jnp.float32)
        ).astype(jnp.bfloat16)


def products_kernel(late, place, scale, *refs):
    out = refs[-1]
    core, y, z = place[0], place[1], place[2]
    n = out.shape[-1]
    row = lax.broadcasted_iota(jnp.int32, (n, n), 0)
    col = lax.broadcasted_iota(jnp.int32, (n, n), 1)

    def product(left, right):
        return lax.dot_general(
            left, right, (((0,), (0,)), ((), ())), preferred_element_type=jnp.float32
        )

    def store(slot, kernel, total):
        out[slot, kernel * n : (kernel + 1) * n] = (total * scale[0]).astype(
            jnp.bfloat16
        )

    packed = (core == 1) & ((z < 8) != (y == 0))
    partner = (core == 0) & (y == 1)

    def four(first, kernel, left, steps):
        total = product(left, steps)
        for j in range(3):
            store(first + j, kernel, total[:, j * n : (j + 1) * n])
        return total[:, 3 * n :]

    if late:
        for kernel in range(2):
            walk, far = refs[kernel : 8 + kernel : 2], refs[8 + kernel]
            steps = jnp.concatenate([w[...] for w in walk], axis=1)
            last = four(0, kernel, far[...], steps)

            @pl.when(jnp.logical_not(packed | partner))
            def _():
                store(3, kernel, last)

        return
    for slot in range(8):
        out[slot, 2 * n : 2 * n + EXTRA] = jnp.zeros((EXTRA, n), jnp.bfloat16)
    for kernel in range(2):
        walk, near = refs[kernel : 10 + kernel : 2], refs[10 + kernel]
        steps = jnp.concatenate([w[...] for w in walk[1:]], axis=1)

        @pl.when(core == 0)
        def _():
            store(7, kernel, four(4, kernel, near[...], steps))

        @pl.when(core == 1)
        def _():
            store(7, kernel, four(4, kernel, walk[0][...], steps))

        @pl.when(partner)
        def _():
            store(3, kernel, product(near[...], walk[0][...]))

        @pl.when(packed)
        def _():
            own = product(walk[0][...], walk[0][...])
            other = product(near[...], near[...])
            high = jnp.where(y == 0, own, other)
            low = jnp.where(y == 0, other, own)
            store(3, kernel, jnp.where(row <= col, high, low))
            diagonal = jnp.sum(jnp.where(row == col, low, 0.0), axis=0, keepdims=True)
            line = lax.broadcasted_iota(jnp.int32, (EXTRA, n), 0)
            extra = out[3, 2 * n : 2 * n + EXTRA].astype(jnp.float32)
            extra = jnp.where(line == kernel, diagonal * scale[0], extra)
            out[3, 2 * n : 2 * n + EXTRA] = extra.astype(jnp.bfloat16)


def place_kernel(total_draws, todo, a, b, feature, gradient):
    n = feature.shape[0]
    row = lax.broadcasted_iota(jnp.int32, (n, n), 0)
    col = lax.broadcasted_iota(jnp.int32, (n, n), 1)
    for kernel, out in enumerate((feature, gradient)):
        block, line = pl.ds(kernel * n, n), pl.ds(2 * n + kernel, 1)
        for half in range(2):
            second, mode = todo[2 * half] == 1, todo[2 * half + 1]
            got = jnp.where(second, b[block, :], a[block, :])
            extra = jnp.where(second, b[line, :], a[line, :])
            turned = got.T
            lower = row > col
            plain = (mode == 0) | ((mode == 2) & (row <= col)) | ((mode == 3) & lower)
            value = jnp.where(plain, got, turned)
            value = jnp.where((mode == 3) & (row == col), extra, value)
            out[:, half * n : (half + 1) * n] = value / total_draws


def on_device(field, backward):
    draws, n = field.shape
    total_draws = draws * 16
    values = jax.ShapeDtypeStruct((draws, n), jnp.bfloat16)
    own = pl.pallas_call(
        features_kernel,
        out_shape=(values, values),
        in_specs=[pl.BlockSpec(memory_space=pltpu.HBM)] * 2,
        out_specs=(VMEM, VMEM),
        scratch_shapes=[
            pltpu.VMEM((draws, n), jnp.bfloat16),
            pltpu.VMEM((draws, n), jnp.bfloat16),
            pltpu.SemaphoreType.DMA((2, PIECES)),
        ],
        compiler_params=pltpu.CompilerParams(vmem_limit_bytes=60 * 1024 * 1024),
    )(field, backward)

    step = [
        (c * 16 + z, c * 16 + (z + 1 - 2 * c) % 16) for c in range(2) for z in range(16)
    ]
    start = chains = [lax.all_gather(part, "c", axis=0, tiled=True) for part in own]
    walk = list(chains)
    for j in range(4):
        chains = [lax.ppermute(chain, ("c", "z"), step) for chain in chains]
        if j == 0:
            start, chains[1] = lax.optimization_barrier((start, chains[1]))
            near = [lax.ppermute(part, "yl", [(0, 1), (1, 0)]) for part in start]
        if j == 2:
            near, chains[1] = lax.optimization_barrier((near, chains[1]))
        walk += chains
    cross = [(0, 2), (1, 3), (2, 1), (3, 0)]
    far = [lax.ppermute(chain, ("c", "yl"), cross) for chain in chains]

    place = jnp.stack([lax.axis_index("c"), lax.axis_index("yl"), lax.axis_index("z")])
    scales = np.exp2(np.arange(8) / 8).astype(np.float32)
    scale = lax.dynamic_slice_in_dim(
        jnp.asarray(scales), lax.axis_index(("yh", "x")), 1
    )
    shape = jax.ShapeDtypeStruct((8, 2 * n + EXTRA, n), jnp.bfloat16)
    cost = pl.CostEstimate(
        flops=32 * n * n * draws, bytes_accessed=28 * n * draws, transcendentals=0
    )
    partial = pl.pallas_call(
        functools.partial(products_kernel, False),
        out_shape=shape,
        in_specs=[SMEM, SMEM] + [VMEM] * 12,
        out_specs=VMEM,
        compiler_params=PARAMS,
        cost_estimate=cost,
    )(place, scale, *walk, *near)
    partial = pl.pallas_call(
        functools.partial(products_kernel, True),
        out_shape=shape,
        in_specs=[SMEM, SMEM] + [VMEM] * 11,
        out_specs=VMEM,
        input_output_aliases={12: 0},
        compiler_params=PARAMS,
        cost_estimate=cost,
    )(place, scale, *walk[2:], *far, partial)
    partial = lax.all_to_all(partial, ("yh", "x"), 0, 0, tiled=True)
    block = jnp.sum(partial.astype(jnp.float32) / scales[:, None, None], axis=0)
    block = block[: 2 * n + 8]

    perms, table = routes()
    a = lax.ppermute(block, AXES, perms[0])
    b = lax.ppermute(block, AXES, perms[1])
    todo = lax.dynamic_index_in_dim(
        jnp.asarray(table), lax.axis_index(AXES), 0, keepdims=False
    )
    out = jax.ShapeDtypeStruct((n, 2 * n), jnp.float32)
    return pl.pallas_call(
        functools.partial(place_kernel, total_draws),
        out_shape=(out, out),
        in_specs=[SMEM, VMEM, VMEM],
        out_specs=(VMEM, VMEM),
        compiler_params=PARAMS,
    )(todo, a, b)


def solution(mesh):
    grid = Mesh(mesh.devices.reshape(SIZES), AXES)
    return jax.shard_map(
        on_device,
        mesh=grid,
        in_specs=(P(("yh", "x", "c"), ("yl", "z")),) * 2,
        out_specs=(P(("yl", "z"), ("yh", "x", "c")),) * 2,
        check_vma=False,
    )
```

```python
import functools

import jax
import jax.numpy as jnp
import numpy as np
from jax import lax
from jax.experimental import pallas as pl
from jax.experimental.pallas import tpu as pltpu
from jax.sharding import Mesh, PartitionSpec as P

AXES = ("yh", "x", "c", "yl", "z")
SIZES = (2, 4, 2, 2, 16)
PIECES = 4
EXTRA = 16
VMEM = pl.BlockSpec(memory_space=pltpu.VMEM)
SMEM = pl.BlockSpec(memory_space=pltpu.SMEM)
PARAMS = pltpu.CompilerParams(vmem_limit_bytes=40 * 1024 * 1024)


def device_index(yh, x, c, yl, z):
    return (((yh * 4 + x) * 2 + c) * 2 + yl) * 16 + z


def home(row_y, row_z, col_y, col_z):
    return device_index(col_y, col_z // 4, col_z % 4 // 2, row_y, row_z), col_z % 2


def homes(yh, x, c, yl, z):
    slot = yh * 4 + x
    if c == 0:
        left, right = (1 - yl, z if slot > 3 else z + 4), (yl, z - slot % 4 - 1)
        if slot == 3 and yl == 1:
            left, right = (0, z), (1, z)
    else:
        left, right = (yl, z if slot > 3 else z - 4), (yl, z + slot % 4 + 1)
        if slot == 3 and (z < 8) != (yl == 0):
            return [home(0, z, 0, z) + (2,), home(1, z, 1, z) + (3,)]
    left, right = (left[0], left[1] % 16), (right[0], right[1] % 16)
    return [home(*left, *right) + (0,), home(*right, *left) + (1,)]


def routes():
    edges = []
    for place in np.ndindex(*SIZES):
        for to, half, mode in homes(*place):
            edges.append((device_index(*place), to, half, mode))
    into = [[] for _ in range(512)]
    for e, edge in enumerate(edges):
        into[edge[1]].append(e)
    turn = [-1] * len(edges)
    for first in range(len(edges)):
        e = first
        while turn[e] < 0:
            turn[e] = 0
            pair = into[edges[e][1]]
            other = pair[0] + pair[1] - e
            turn[other] = 1
            e = other ^ 1
    perms = [[], []]
    table = np.zeros((512, 4), np.int32)
    for e, (source, to, half, mode) in enumerate(edges):
        perms[turn[e]].append((source, to))
        table[to, 2 * half] = turn[e]
        table[to, 2 * half + 1] = mode
    return perms, table


def features_kernel(field, backward, activity, signal, both, f, b, sems):
    rows = field.shape[0] // PIECES
    copies = []
    for piece in range(PIECES):
        part = pl.ds(piece * rows, rows)
        copies.append(
            [
                pltpu.make_async_copy(src.at[part], dst.at[part], sems.at[i, piece])
                for i, (src, dst) in enumerate(((field, f), (backward, b)))
            ]
        )
        for copy in copies[-1]:
            copy.start()
    for piece in range(PIECES):
        part = pl.ds(piece * rows, rows)
        for copy in copies[piece]:
            copy.wait()
        wide = jnp.tanh(f[part, :].astype(jnp.float32))
        gated = (1.0 - wide * wide) * b[part, :].astype(jnp.float32)
        for i, (out, value) in enumerate(((activity, wide), (signal, gated))):
            out[part, :] = value.astype(jnp.bfloat16)
            both[i, part, :] = value.astype(jnp.bfloat16)


def products_kernel(late, place, scale, *refs):
    out = refs[-1]
    core, y, z = place[0], place[1], place[2]
    n = out.shape[-1]
    row = lax.broadcasted_iota(jnp.int32, (n, n), 0)
    col = lax.broadcasted_iota(jnp.int32, (n, n), 1)

    def product(left, right):
        return lax.dot_general(
            left, right, (((0,), (0,)), ((), ())), preferred_element_type=jnp.float32
        )

    def store(slot, kernel, total):
        out[slot, kernel * n : (kernel + 1) * n] = (total * scale[0]).astype(
            jnp.bfloat16
        )

    packed = (core == 1) & ((z < 8) != (y == 0))
    partner = (core == 0) & (y == 1)

    def four(first, kernel, left, steps):
        total = product(left, steps)
        for j in range(3):
            store(first + j, kernel, total[:, j * n : (j + 1) * n])
        return total[:, 3 * n :]

    if late:
        for kernel in range(2):
            walk, far = refs[kernel : 8 + kernel : 2], refs[8 + kernel]
            steps = jnp.concatenate([w[...] for w in walk], axis=1)
            last = four(0, kernel, far[...], steps)

            @pl.when(jnp.logical_not(packed | partner))
            def _():
                store(3, kernel, last)

        return
    for slot in range(8):
        out[slot, 2 * n : 2 * n + EXTRA] = jnp.zeros((EXTRA, n), jnp.bfloat16)
    for kernel in range(2):
        walk, gathered = refs[kernel : 10 + kernel : 2], refs[10]
        rows = gathered.shape[1] // 4
        near = [
            gathered[kernel, pl.ds(pl.multiple_of((2 * c + 1 - y) * rows, rows), rows)]
            for c in range(2)
        ]
        near = jnp.concatenate(near, axis=0)
        steps = jnp.concatenate([w[...] for w in walk[1:]], axis=1)

        @pl.when(core == 0)
        def _():
            store(7, kernel, four(4, kernel, near, steps))

        @pl.when(core == 1)
        def _():
            store(7, kernel, four(4, kernel, walk[0][...], steps))

        @pl.when(partner)
        def _():
            store(3, kernel, product(near, walk[0][...]))

        @pl.when(packed)
        def _():
            own = product(walk[0][...], walk[0][...])
            other = product(near, near)
            high = jnp.where(y == 0, own, other)
            low = jnp.where(y == 0, other, own)
            store(3, kernel, jnp.where(row <= col, high, low))
            diagonal = jnp.sum(jnp.where(row == col, low, 0.0), axis=0, keepdims=True)
            line = lax.broadcasted_iota(jnp.int32, (EXTRA, n), 0)
            extra = out[3, 2 * n : 2 * n + EXTRA].astype(jnp.float32)
            extra = jnp.where(line == kernel, diagonal * scale[0], extra)
            out[3, 2 * n : 2 * n + EXTRA] = extra.astype(jnp.bfloat16)


def place_kernel(total_draws, todo, a, b, feature, gradient):
    n = feature.shape[0]
    row = lax.broadcasted_iota(jnp.int32, (n, n), 0)
    col = lax.broadcasted_iota(jnp.int32, (n, n), 1)
    for kernel, out in enumerate((feature, gradient)):
        block, line = pl.ds(kernel * n, n), pl.ds(2 * n + kernel, 1)
        for half in range(2):
            second, mode = todo[2 * half] == 1, todo[2 * half + 1]
            got = jnp.where(second, b[block, :], a[block, :])
            extra = jnp.where(second, b[line, :], a[line, :])
            turned = got.T
            lower = row > col
            plain = (mode == 0) | ((mode == 2) & (row <= col)) | ((mode == 3) & lower)
            value = jnp.where(plain, got, turned)
            value = jnp.where((mode == 3) & (row == col), extra, value)
            out[:, half * n : (half + 1) * n] = value / total_draws


def on_device(field, backward):
    draws, n = field.shape
    total_draws = draws * 16
    values = jax.ShapeDtypeStruct((draws, n), jnp.bfloat16)
    *own, both = pl.pallas_call(
        features_kernel,
        out_shape=(values, values, jax.ShapeDtypeStruct((2, draws, n), jnp.bfloat16)),
        in_specs=[pl.BlockSpec(memory_space=pltpu.HBM)] * 2,
        out_specs=(VMEM,) * 3,
        scratch_shapes=[
            pltpu.VMEM((draws, n), jnp.bfloat16),
            pltpu.VMEM((draws, n), jnp.bfloat16),
            pltpu.SemaphoreType.DMA((2, PIECES)),
        ],
        compiler_params=pltpu.CompilerParams(vmem_limit_bytes=60 * 1024 * 1024),
    )(field, backward)

    step = [
        (c * 16 + z, c * 16 + (z + 1 - 2 * c) % 16) for c in range(2) for z in range(16)
    ]
    chains = [lax.all_gather(part, "c", axis=0, tiled=True) for part in own]
    near = lax.all_gather(both, ("c", "yl"), axis=1, tiled=True)
    walk = list(chains)
    for _ in range(4):
        chains = [lax.ppermute(chain, ("c", "z"), step) for chain in chains]
        walk += chains
    cross = [(0, 2), (1, 3), (2, 1), (3, 0)]
    far = [lax.ppermute(chain, ("c", "yl"), cross) for chain in chains]

    place = jnp.stack([lax.axis_index("c"), lax.axis_index("yl"), lax.axis_index("z")])
    scales = np.exp2(np.arange(8) / 8).astype(np.float32)
    scale = lax.dynamic_slice_in_dim(
        jnp.asarray(scales), lax.axis_index(("yh", "x")), 1
    )
    shape = jax.ShapeDtypeStruct((8, 2 * n + EXTRA, n), jnp.bfloat16)
    cost = pl.CostEstimate(
        flops=32 * n * n * draws, bytes_accessed=28 * n * draws, transcendentals=0
    )
    partial = pl.pallas_call(
        functools.partial(products_kernel, False),
        out_shape=shape,
        in_specs=[SMEM, SMEM] + [VMEM] * 11,
        out_specs=VMEM,
        compiler_params=PARAMS,
        cost_estimate=cost,
    )(place, scale, *walk, near)
    partial = pl.pallas_call(
        functools.partial(products_kernel, True),
        out_shape=shape,
        in_specs=[SMEM, SMEM] + [VMEM] * 11,
        out_specs=VMEM,
        input_output_aliases={12: 0},
        compiler_params=PARAMS,
        cost_estimate=cost,
    )(place, scale, *walk[2:], *far, partial)
    partial = lax.all_to_all(partial, ("yh", "x"), 0, 0, tiled=True)
    block = jnp.sum(partial.astype(jnp.float32) / scales[:, None, None], axis=0)
    block = block[: 2 * n + 8]

    perms, table = routes()
    a = lax.ppermute(block, AXES, perms[0])
    b = lax.ppermute(block, AXES, perms[1])
    todo = lax.dynamic_index_in_dim(
        jnp.asarray(table), lax.axis_index(AXES), 0, keepdims=False
    )
    out = jax.ShapeDtypeStruct((n, 2 * n), jnp.float32)
    return pl.pallas_call(
        functools.partial(place_kernel, total_draws),
        out_shape=(out, out),
        in_specs=[SMEM, VMEM, VMEM],
        out_specs=(VMEM, VMEM),
        compiler_params=PARAMS,
    )(todo, a, b)


def solution(mesh):
    grid = Mesh(mesh.devices.reshape(SIZES), AXES)
    return jax.shard_map(
        on_device,
        mesh=grid,
        in_specs=(P(("yh", "x", "c"), ("yl", "z")),) * 2,
        out_specs=(P(("yl", "z"), ("yh", "x", "c")),) * 2,
        check_vma=False,
    )
```

```python
import functools

import jax
import jax.numpy as jnp
import numpy as np
from jax import lax
from jax.experimental import pallas as pl
from jax.experimental.pallas import tpu as pltpu
from jax.sharding import Mesh, PartitionSpec as P

AXES = ("yh", "x", "c", "yl", "z")
SIZES = (2, 4, 2, 2, 16)
PIECES = 4
EXTRA = 16
VMEM = pl.BlockSpec(memory_space=pltpu.VMEM)
SMEM = pl.BlockSpec(memory_space=pltpu.SMEM)
PARAMS = pltpu.CompilerParams(vmem_limit_bytes=40 * 1024 * 1024)


def device_index(yh, x, c, yl, z):
    return (((yh * 4 + x) * 2 + c) * 2 + yl) * 16 + z


def home(row_y, row_z, col_y, col_z):
    return device_index(col_y, col_z // 4, col_z % 4 // 2, row_y, row_z), col_z % 2


def homes(yh, x, c, yl, z):
    slot = yh * 4 + x
    if c == 0:
        left, right = (1 - yl, z if slot > 3 else z + 4), (yl, z - slot % 4 - 1)
        if slot == 3 and yl == 1:
            left, right = (0, z), (1, z)
    else:
        left, right = (yl, z if slot > 3 else z - 4), (yl, z + slot % 4 + 1)
        if slot == 3 and (z < 8) != (yl == 0):
            return [home(0, z, 0, z) + (2,), home(1, z, 1, z) + (3,)]
    left, right = (left[0], left[1] % 16), (right[0], right[1] % 16)
    return [home(*left, *right) + (0,), home(*right, *left) + (1,)]


def routes():
    edges = []
    for place in np.ndindex(*SIZES):
        for to, half, mode in homes(*place):
            edges.append((device_index(*place), to, half, mode))
    into = [[] for _ in range(512)]
    for e, edge in enumerate(edges):
        into[edge[1]].append(e)
    turn = [-1] * len(edges)
    for first in range(len(edges)):
        e = first
        while turn[e] < 0:
            turn[e] = 0
            pair = into[edges[e][1]]
            other = pair[0] + pair[1] - e
            turn[other] = 1
            e = other ^ 1
    perms = [[], []]
    table = np.zeros((512, 4), np.int32)
    for e, (source, to, half, mode) in enumerate(edges):
        perms[turn[e]].append((source, to))
        table[to, 2 * half] = turn[e]
        table[to, 2 * half + 1] = mode
    return perms, table


def features_kernel(field, backward, both, f, b, sems):
    rows = field.shape[0] // PIECES
    copies = []
    for piece in range(PIECES):
        part = pl.ds(piece * rows, rows)
        copies.append(
            [
                pltpu.make_async_copy(src.at[part], dst.at[part], sems.at[i, piece])
                for i, (src, dst) in enumerate(((field, f), (backward, b)))
            ]
        )
        for copy in copies[-1]:
            copy.start()
    for piece in range(PIECES):
        part = pl.ds(piece * rows, rows)
        for copy in copies[piece]:
            copy.wait()
        wide = jnp.tanh(f[part, :].astype(jnp.float32))
        gated = (1.0 - wide * wide) * b[part, :].astype(jnp.float32)
        both[0, part, :] = wide.astype(jnp.bfloat16)
        both[1, part, :] = gated.astype(jnp.bfloat16)


def product(left, right):
    return lax.dot_general(
        left, right, (((0,), (0,)), ((), ())), preferred_element_type=jnp.float32
    )


def store(out, scale, slot, kernel, total):
    n = out.shape[-1]
    for j in range(total.shape[1] // n):
        block = total[:, j * n : (j + 1) * n] * scale[0]
        out[slot + j, kernel * n : (kernel + 1) * n] = block.astype(jnp.bfloat16)


def cases(place):
    core, y, z = place[0], place[1], place[2]
    return (core == 1) & ((z < 8) != (y == 0)), (core == 0) & (y == 1)


def near_kernel(place, scale, *refs):
    first, second, near, (out, steps) = refs[0:5], refs[5:10], refs[10:12], refs[12:]
    core, y = place[0], place[1]
    packed, partner = cases(place)
    n = out.shape[-1]
    rows = near[0].shape[1]
    for slot in range(8):
        out[slot, 2 * n : 2 * n + EXTRA] = jnp.zeros((EXTRA, n), jnp.bfloat16)
    for kernel in range(2):
        for i, chain in enumerate((first, second)):
            for j in range(4):
                steps[kernel, i * rows : (i + 1) * rows, j * n : (j + 1) * n] = chain[
                    j + 1
                ][kernel]

        def own(kernel=kernel):
            return jnp.concatenate([first[0][kernel], second[0][kernel]], axis=0)

        def other(kernel=kernel):
            return jnp.concatenate([near[0][kernel], near[1][kernel]], axis=0)

        @pl.when(core == 0)
        def _():
            store(out, scale, 4, kernel, product(other(), steps[kernel]))

        @pl.when(core == 1)
        def _():
            store(out, scale, 4, kernel, product(own(), steps[kernel]))

        @pl.when(partner)
        def _():
            store(out, scale, 3, kernel, product(other(), own()))

        @pl.when(packed)
        def _():
            mine, yours = product(own(), own()), product(other(), other())
            high = jnp.where(y == 0, mine, yours)
            low = jnp.where(y == 0, yours, mine)
            row = lax.broadcasted_iota(jnp.int32, (n, n), 0)
            col = lax.broadcasted_iota(jnp.int32, (n, n), 1)
            store(out, scale, 3, kernel, jnp.where(row <= col, high, low))
            diagonal = jnp.sum(jnp.where(row == col, low, 0.0), axis=0, keepdims=True)
            line = lax.broadcasted_iota(jnp.int32, (EXTRA, n), 0)
            extra = out[3, 2 * n : 2 * n + EXTRA].astype(jnp.float32)
            extra = jnp.where(line == kernel, diagonal * scale[0], extra)
            out[3, 2 * n : 2 * n + EXTRA] = extra.astype(jnp.bfloat16)


def far_kernel(place, scale, steps, first, second, _, out):
    packed, partner = cases(place)
    n = out.shape[-1]
    for kernel in range(2):
        far = jnp.concatenate([first[kernel], second[kernel]], axis=0)
        total = product(far, steps[kernel])
        store(out, scale, 0, kernel, total[:, : 3 * n])

        @pl.when(jnp.logical_not(packed | partner))
        def _():
            store(out, scale, 3, kernel, total[:, 3 * n :])


def place_kernel(total_draws, todo, a, b, feature, gradient):
    n = feature.shape[0]
    row = lax.broadcasted_iota(jnp.int32, (n, n), 0)
    col = lax.broadcasted_iota(jnp.int32, (n, n), 1)
    for kernel, out in enumerate((feature, gradient)):
        block, line = pl.ds(kernel * n, n), pl.ds(2 * n + kernel, 1)
        for half in range(2):
            second, mode = todo[2 * half] == 1, todo[2 * half + 1]
            got = jnp.where(second, b[block, :], a[block, :])
            extra = jnp.where(second, b[line, :], a[line, :])
            turned = got.T
            lower = row > col
            plain = (mode == 0) | ((mode == 2) & (row <= col)) | ((mode == 3) & lower)
            value = jnp.where(plain, got, turned)
            value = jnp.where((mode == 3) & (row == col), extra, value)
            out[:, half * n : (half + 1) * n] = value / total_draws


def on_device(field, backward):
    draws, n = field.shape
    total_draws = draws * 16
    both = pl.pallas_call(
        features_kernel,
        out_shape=jax.ShapeDtypeStruct((2, draws, n), jnp.bfloat16),
        in_specs=[pl.BlockSpec(memory_space=pltpu.HBM)] * 2,
        out_specs=VMEM,
        scratch_shapes=[
            pltpu.VMEM((draws, n), jnp.bfloat16),
            pltpu.VMEM((draws, n), jnp.bfloat16),
            pltpu.SemaphoreType.DMA((2, PIECES)),
        ],
        compiler_params=pltpu.CompilerParams(vmem_limit_bytes=60 * 1024 * 1024),
    )(field, backward)

    swap = [(0, 1), (1, 0)]
    step = [
        (c * 16 + z, c * 16 + (z + 1 - 2 * c) % 16) for c in range(2) for z in range(16)
    ]
    chains = [both, lax.ppermute(both, "c", swap)]
    walk = [[chain] for chain in chains]
    near = [both]
    for j in range(4):
        chains = [lax.ppermute(chain, ("c", "z"), step) for chain in chains]
        if j == 0:
            near[0], chains[1] = lax.optimization_barrier((near[0], chains[1]))
            near = [lax.ppermute(near[0], "yl", swap)]
        if j == 2:
            near[0], chains[1] = lax.optimization_barrier((near[0], chains[1]))
            near.append(lax.ppermute(near[0], "c", swap))
        if j == 3:
            near[1], chains[1] = lax.optimization_barrier((near[1], chains[1]))
        for chain, blocks in zip(chains, walk):
            blocks.append(chain)
    cross = [(0, 2), (1, 3), (2, 1), (3, 0)]
    far = [lax.ppermute(chain, ("c", "yl"), cross) for chain in chains]

    place = jnp.stack([lax.axis_index("c"), lax.axis_index("yl"), lax.axis_index("z")])
    scales = np.exp2(np.arange(8) / 8).astype(np.float32)
    scale = lax.dynamic_slice_in_dim(
        jnp.asarray(scales), lax.axis_index(("yh", "x")), 1
    )
    shape = jax.ShapeDtypeStruct((8, 2 * n + EXTRA, n), jnp.bfloat16)
    cost = pl.CostEstimate(
        flops=32 * n * n * draws, bytes_accessed=28 * n * draws, transcendentals=0
    )
    partial, steps = pl.pallas_call(
        near_kernel,
        out_shape=(shape, jax.ShapeDtypeStruct((2, 2 * draws, 4 * n), jnp.bfloat16)),
        in_specs=[SMEM, SMEM] + [VMEM] * 12,
        out_specs=(VMEM, VMEM),
        compiler_params=PARAMS,
        cost_estimate=cost,
    )(place, scale, *walk[0], *walk[1], *near)
    partial = pl.pallas_call(
        far_kernel,
        out_shape=shape,
        in_specs=[SMEM, SMEM] + [VMEM] * 4,
        out_specs=VMEM,
        input_output_aliases={5: 0},
        compiler_params=PARAMS,
        cost_estimate=cost,
    )(place, scale, steps, far[1], far[0], partial)
    partial = lax.all_to_all(partial, ("yh", "x"), 0, 0, tiled=True)
    block = jnp.sum(partial.astype(jnp.float32) / scales[:, None, None], axis=0)
    block = block[: 2 * n + 8]

    perms, table = routes()
    a = lax.ppermute(block, AXES, perms[0])
    b = lax.ppermute(block, AXES, perms[1])
    todo = lax.dynamic_index_in_dim(
        jnp.asarray(table), lax.axis_index(AXES), 0, keepdims=False
    )
    out = jax.ShapeDtypeStruct((n, 2 * n), jnp.float32)
    return pl.pallas_call(
        functools.partial(place_kernel, total_draws),
        out_shape=(out, out),
        in_specs=[SMEM, VMEM, VMEM],
        out_specs=(VMEM, VMEM),
        compiler_params=PARAMS,
    )(todo, a, b)


def solution(mesh):
    grid = Mesh(mesh.devices.reshape(SIZES), AXES)
    return jax.shard_map(
        on_device,
        mesh=grid,
        in_specs=(P(("yh", "x", "c"), ("yl", "z")),) * 2,
        out_specs=(P(("yl", "z"), ("yh", "x", "c")),) * 2,
        check_vma=False,
    )
```

```python
import functools

import jax
import jax.numpy as jnp
import numpy as np
from jax import lax
from jax.experimental import pallas as pl
from jax.experimental.pallas import tpu as pltpu
from jax.sharding import Mesh, PartitionSpec as P

AXES = ("yh", "x", "c", "yl", "z")
SIZES = (2, 4, 2, 2, 16)
PIECES = 4
EXTRA = 16
VMEM = pl.BlockSpec(memory_space=pltpu.VMEM)
SMEM = pl.BlockSpec(memory_space=pltpu.SMEM)
PARAMS = pltpu.CompilerParams(vmem_limit_bytes=40 * 1024 * 1024)


def device_index(yh, x, c, yl, z):
    return (((yh * 4 + x) * 2 + c) * 2 + yl) * 16 + z


def home(row_y, row_z, col_y, col_z):
    return device_index(col_y, col_z // 4, col_z % 4 // 2, row_y, row_z), col_z % 2


def homes(yh, x, c, yl, z):
    slot = yh * 4 + x
    if c == 0:
        left, right = (1 - yl, z if slot > 3 else z + 4), (yl, z - slot % 4 - 1)
        if slot == 3 and yl == 1:
            left, right = (0, z), (1, z)
    else:
        left, right = (yl, z if slot > 3 else z - 4), (yl, z + slot % 4 + 1)
        if slot == 3 and (z < 8) != (yl == 0):
            return [home(0, z, 0, z) + (2,), home(1, z, 1, z) + (3,)]
    left, right = (left[0], left[1] % 16), (right[0], right[1] % 16)
    return [home(*left, *right) + (0,), home(*right, *left) + (1,)]


def routes():
    edges = []
    for place in np.ndindex(*SIZES):
        for to, half, mode in homes(*place):
            edges.append((device_index(*place), to, half, mode))
    into = [[] for _ in range(512)]
    for e, edge in enumerate(edges):
        into[edge[1]].append(e)
    turn = [-1] * len(edges)
    for first in range(len(edges)):
        e = first
        while turn[e] < 0:
            turn[e] = 0
            pair = into[edges[e][1]]
            other = pair[0] + pair[1] - e
            turn[other] = 1
            e = other ^ 1
    perms = [[], []]
    table = np.zeros((512, 4), np.int32)
    for e, (source, to, half, mode) in enumerate(edges):
        perms[turn[e]].append((source, to))
        table[to, 2 * half] = turn[e]
        table[to, 2 * half + 1] = mode
    return perms, table


def features_kernel(field, backward, both, f, b, sems):
    rows = field.shape[0] // PIECES
    copies = []
    for piece in range(PIECES):
        part = pl.ds(piece * rows, rows)
        copies.append(
            [
                pltpu.make_async_copy(src.at[part], dst.at[part], sems.at[i, piece])
                for i, (src, dst) in enumerate(((field, f), (backward, b)))
            ]
        )
        for copy in copies[-1]:
            copy.start()
    for piece in range(PIECES):
        part = pl.ds(piece * rows, rows)
        for copy in copies[piece]:
            copy.wait()
        wide = jnp.tanh(f[part, :].astype(jnp.float32))
        gated = (1.0 - wide * wide) * b[part, :].astype(jnp.float32)
        both[0, part, :] = wide.astype(jnp.bfloat16)
        both[1, part, :] = gated.astype(jnp.bfloat16)


def product(left, right):
    return lax.dot_general(
        left, right, (((0,), (0,)), ((), ())), preferred_element_type=jnp.float32
    )


def store(out, scale, slot, kernel, total):
    n = out.shape[-1]
    for j in range(total.shape[1] // n):
        block = total[:, j * n : (j + 1) * n] * scale
        out[slot + j, kernel * n : (kernel + 1) * n] = block.astype(jnp.bfloat16)


def cases(place):
    core, y, z = place[0], place[1], place[2]
    return (core == 1) & ((z < 8) != (y == 0)), (core == 0) & (y == 1)


def early_kernel(place, scales, *refs):
    first, second, near, (out, left, steps) = refs[0:4], refs[4:8], refs[8:10], refs[10:]
    core, y, scale = place[0], place[1], scales[place[3]]
    packed, partner = cases(place)
    n = out.shape[-1]
    rows = near[0].shape[1]
    for slot in range(8):
        out[slot, 2 * n : 2 * n + EXTRA] = jnp.zeros((EXTRA, n), jnp.bfloat16)
    for kernel in range(2):
        for i, chain in enumerate((first, second)):
            part = pl.ds(i * rows, rows)
            for j in range(3):
                steps[kernel, part, j * n : (j + 1) * n] = chain[j + 1][kernel]

        def own(kernel=kernel):
            return jnp.concatenate([first[0][kernel], second[0][kernel]], axis=0)

        def other(kernel=kernel):
            return jnp.concatenate([near[0][kernel], near[1][kernel]], axis=0)

        @pl.when(core == 0)
        def _():
            left[kernel] = other()

        @pl.when(core == 1)
        def _():
            left[kernel] = own()

        total = product(left[kernel], steps[kernel, :, 0 : 3 * n])
        store(out, scale, 4, kernel, total)

        @pl.when(partner)
        def _():
            store(out, scale, 3, kernel, product(other(), own()))

        @pl.when(packed)
        def _():
            mine, yours = product(own(), own()), product(other(), other())
            high = jnp.where(y == 0, mine, yours)
            low = jnp.where(y == 0, yours, mine)
            row = lax.broadcasted_iota(jnp.int32, (n, n), 0)
            col = lax.broadcasted_iota(jnp.int32, (n, n), 1)
            store(out, scale, 3, kernel, jnp.where(row <= col, high, low))
            diagonal = jnp.sum(jnp.where(row == col, low, 0.0), axis=0, keepdims=True)
            line = lax.broadcasted_iota(jnp.int32, (EXTRA, n), 0)
            extra = out[3, 2 * n : 2 * n + EXTRA].astype(jnp.float32)
            extra = jnp.where(line == kernel, diagonal * scale, extra)
            out[3, 2 * n : 2 * n + EXTRA] = extra.astype(jnp.bfloat16)


def middle_kernel(place, scales, first, second, far, left, _, __, out, steps, total):
    scale = scales[place[3]]
    n = out.shape[-1]
    rows = far.shape[1]
    for kernel in range(2):
        for i, chain in enumerate((first, second)):
            steps[kernel, i * rows : (i + 1) * rows, 3 * n :] = chain[kernel]
        total[kernel] = product(far[kernel], steps[kernel, rows:])
        last = product(left[kernel], steps[kernel, :, 3 * n :])
        store(out, scale, 7, kernel, last)


def late_kernel(place, scales, far, steps, part, _, out):
    scale = scales[place[3]]
    packed, partner = cases(place)
    n = out.shape[-1]
    rows = far.shape[1]
    for kernel in range(2):
        total = part[kernel] + product(far[kernel], steps[kernel, 0:rows])
        store(out, scale, 0, kernel, total[:, : 3 * n])

        @pl.when(jnp.logical_not(packed | partner))
        def _():
            store(out, scale, 3, kernel, total[:, 3 * n :])


def place_kernel(total_draws, todo, a, b, feature, gradient):
    n = feature.shape[0]
    row = lax.broadcasted_iota(jnp.int32, (n, n), 0)
    col = lax.broadcasted_iota(jnp.int32, (n, n), 1)
    for kernel, out in enumerate((feature, gradient)):
        block, line = pl.ds(kernel * n, n), pl.ds(2 * n + kernel, 1)
        for half in range(2):
            second, mode = todo[2 * half] == 1, todo[2 * half + 1]
            got = jnp.where(second, b[block, :], a[block, :])
            extra = jnp.where(second, b[line, :], a[line, :])
            turned = got.T
            lower = row > col
            plain = (mode == 0) | ((mode == 2) & (row <= col)) | ((mode == 3) & lower)
            value = jnp.where(plain, got, turned)
            value = jnp.where((mode == 3) & (row == col), extra, value)
            out[:, half * n : (half + 1) * n] = value / total_draws


def on_device(field, backward):
    draws, n = field.shape
    total_draws = draws * 16
    both = pl.pallas_call(
        features_kernel,
        out_shape=jax.ShapeDtypeStruct((2, draws, n), jnp.bfloat16),
        in_specs=[pl.BlockSpec(memory_space=pltpu.HBM)] * 2,
        out_specs=VMEM,
        scratch_shapes=[
            pltpu.VMEM((draws, n), jnp.bfloat16),
            pltpu.VMEM((draws, n), jnp.bfloat16),
            pltpu.SemaphoreType.DMA((2, PIECES)),
        ],
        compiler_params=pltpu.CompilerParams(vmem_limit_bytes=60 * 1024 * 1024),
    )(field, backward)

    step, first_step = [], []
    for c in range(2):
        for z in range(16):
            step.append((c * 16 + z, c * 16 + (z + 1 - 2 * c) % 16))
            first_step.append((c * 16 + z, (1 - c) * 16 + (z + 2 * c - 1) % 16))
    place = jnp.stack([lax.axis_index(a) for a in ("c", "yl", "z", ("yh", "x"))])
    scales = np.exp2(np.arange(8) / 8).astype(np.float32)
    shape = jax.ShapeDtypeStruct((8, 2 * n + EXTRA, n), jnp.bfloat16)
    left_shape = jax.ShapeDtypeStruct((2, 2 * draws, n), jnp.bfloat16)
    steps_shape = jax.ShapeDtypeStruct((2, 2 * draws, 4 * n), jnp.bfloat16)
    total_shape = jax.ShapeDtypeStruct((2, n, 4 * n), jnp.float32)

    def call(kernel, out_shape, *args, aliases={}, flops=1):
        return pl.pallas_call(
            kernel,
            out_shape=out_shape,
            in_specs=[SMEM, SMEM] + [VMEM] * len(args),
            out_specs=jax.tree.map(lambda _: VMEM, out_shape),
            input_output_aliases=aliases,
            compiler_params=PARAMS,
            cost_estimate=pl.CostEstimate(
                flops=flops * 8 * n * n * draws,
                bytes_accessed=28 * n * draws,
                transcendentals=0,
            ),
        )(place, jnp.asarray(scales), *args)

    chains = [
        lax.ppermute(both, ("c", "z"), step),
        lax.ppermute(both, ("c", "z"), first_step),
    ]
    walk = [[], []]
    for j in range(4):
        if j:
            chains = [lax.ppermute(chain, ("c", "z"), step) for chain in chains]
        if j == 0:
            own, chains[1] = lax.optimization_barrier((both, chains[1]))
            near = [lax.ppermute(own, "yl", [(0, 1), (1, 0)])]
        if j == 1:
            own, near[0], chains[1] = lax.optimization_barrier(
                (own, near[0], chains[1])
            )
            near.append(
                lax.ppermute(own, ("c", "yl"), [(0, 3), (1, 2), (2, 1), (3, 0)])
            )
            other = lax.ppermute(own, "c", [(0, 1), (1, 0)])
        if j == 2:
            near[1], chains[1] = lax.optimization_barrier((near[1], chains[1]))
        if j == 3:
            partial, left, steps = call(
                early_kernel,
                (shape, left_shape, steps_shape),
                *(both, *walk[0], other, *walk[1], *near),
                flops=4,
            )
            partial, chains[0] = lax.optimization_barrier((partial, chains[0]))
        for chain, blocks in zip(chains, walk):
            blocks.append(chain)
    cross = [(0, 2), (1, 3), (2, 1), (3, 0)]
    far = [lax.ppermute(chain, ("c", "yl"), cross) for chain in chains]

    partial, steps, total = call(
        middle_kernel,
        (shape, steps_shape, total_shape),
        *(*chains, far[0], left, partial, steps),
        aliases={6: 0, 7: 1},
        flops=3,
    )
    partial = call(late_kernel, shape, far[1], steps, total, partial, aliases={5: 0}, flops=2)
    partial = lax.all_to_all(partial, ("yh", "x"), 0, 0, tiled=True)
    block = jnp.sum(partial.astype(jnp.float32) / scales[:, None, None], axis=0)
    block = block[: 2 * n + 8]

    perms, table = routes()
    a = lax.ppermute(block, AXES, perms[0])
    b = lax.ppermute(block, AXES, perms[1])
    todo = lax.dynamic_index_in_dim(
        jnp.asarray(table), lax.axis_index(AXES), 0, keepdims=False
    )
    out = jax.ShapeDtypeStruct((n, 2 * n), jnp.float32)
    return pl.pallas_call(
        functools.partial(place_kernel, total_draws),
        out_shape=(out, out),
        in_specs=[SMEM, VMEM, VMEM],
        out_specs=(VMEM, VMEM),
        compiler_params=PARAMS,
    )(todo, a, b)


def solution(mesh):
    grid = Mesh(mesh.devices.reshape(SIZES), AXES)
    return jax.shard_map(
        on_device,
        mesh=grid,
        in_specs=(P(("yh", "x", "c"), ("yl", "z")),) * 2,
        out_specs=(P(("yl", "z"), ("yh", "x", "c")),) * 2,
        check_vma=False,
    )
```

```python
import functools

import jax
import jax.numpy as jnp
import numpy as np
from jax import lax
from jax.experimental import pallas as pl
from jax.experimental.pallas import tpu as pltpu
from jax.sharding import Mesh, PartitionSpec as P

AXES = ("yh", "x", "c", "yl", "z")
SIZES = (2, 4, 2, 2, 16)
PIECES = 4
EXTRA = 16
VMEM = pl.BlockSpec(memory_space=pltpu.VMEM)
SMEM = pl.BlockSpec(memory_space=pltpu.SMEM)
PARAMS = pltpu.CompilerParams(vmem_limit_bytes=40 * 1024 * 1024)


def device_index(yh, x, c, yl, z):
    return (((yh * 4 + x) * 2 + c) * 2 + yl) * 16 + z


def home(row_y, row_z, col_y, col_z):
    return device_index(col_y, col_z // 4, col_z % 4 // 2, row_y, row_z), col_z % 2


def homes(yh, x, c, yl, z):
    slot = yh * 4 + x
    if c == 0:
        left = (yl, z) if slot > 3 else (1 - yl, z + 4)
        right = (yl, z - slot % 4 - 1)
        if slot == 3 and yl == 1:
            right = (yl, z)
    else:
        left = (1 - yl, z) if slot > 3 else (yl, z - 4)
        right = (yl, z + slot % 4 + 1)
        if slot == 3 and (z < 8) != (yl == 0):
            return [home(0, z, 0, z) + (2,), home(1, z, 1, z) + (3,)]
        if slot == 7 and yl == 0:
            right = (yl, z)
    left, right = (left[0], left[1] % 16), (right[0], right[1] % 16)
    return [home(*left, *right) + (0,), home(*right, *left) + (1,)]


def routes():
    edges = []
    for place in np.ndindex(*SIZES):
        for to, half, mode in homes(*place):
            edges.append((device_index(*place), to, half, mode))
    into = [[] for _ in range(512)]
    for e, edge in enumerate(edges):
        into[edge[1]].append(e)
    turn = [-1] * len(edges)
    for first in range(len(edges)):
        e = first
        while turn[e] < 0:
            turn[e] = 0
            pair = into[edges[e][1]]
            other = pair[0] + pair[1] - e
            turn[other] = 1
            e = other ^ 1
    perms = [[], []]
    table = np.zeros((512, 4), np.int32)
    for e, (source, to, half, mode) in enumerate(edges):
        perms[turn[e]].append((source, to))
        table[to, 2 * half] = turn[e]
        table[to, 2 * half + 1] = mode
    return perms, table


def features_kernel(field, backward, both, f, b, sems):
    rows = field.shape[0] // PIECES
    copies = []
    for piece in range(PIECES):
        part = pl.ds(piece * rows, rows)
        copies.append(
            [
                pltpu.make_async_copy(src.at[part], dst.at[part], sems.at[i, piece])
                for i, (src, dst) in enumerate(((field, f), (backward, b)))
            ]
        )
        for copy in copies[-1]:
            copy.start()
    for piece in range(PIECES):
        part = pl.ds(piece * rows, rows)
        for copy in copies[piece]:
            copy.wait()
        wide = jnp.tanh(f[part, :].astype(jnp.float32))
        gated = (1.0 - wide * wide) * b[part, :].astype(jnp.float32)
        both[0, part, :] = wide.astype(jnp.bfloat16)
        both[1, part, :] = gated.astype(jnp.bfloat16)


def product(left, right):
    return lax.dot_general(
        left, right, (((0,), (0,)), ((), ())), preferred_element_type=jnp.float32
    )


def store(out, scale, slot, kernel, total):
    n = out.shape[-1]
    for j in range(total.shape[1] // n):
        block = total[:, j * n : (j + 1) * n] * scale
        out[slot + j, kernel * n : (kernel + 1) * n] = block.astype(jnp.bfloat16)


def cases(place):
    core, y, z = place[0], place[1], place[2]
    return (core == 1) & ((z < 8) != (y == 0)), (core == 1) & (y == 0), (core == 0) & (y == 1)


def early_kernel(place, scales, *refs):
    first, second, near, (out, left, steps) = refs[0:4], refs[4:8], refs[8:10], refs[10:]
    core, y, scale = place[0], place[1], scales[place[3]]
    packed, same, _ = cases(place)
    n = out.shape[-1]
    rows = near[0].shape[1]
    for slot in range(8):
        out[slot, 2 * n : 2 * n + EXTRA] = jnp.zeros((EXTRA, n), jnp.bfloat16)
    for kernel in range(2):
        for i, chain in enumerate((first, second)):
            part = pl.ds(i * rows, rows)
            for j in range(3):
                steps[kernel, part, j * n : (j + 1) * n] = chain[j + 1][kernel]

        def own(kernel=kernel):
            return jnp.concatenate([first[0][kernel], second[0][kernel]], axis=0)

        def other(kernel=kernel):
            return jnp.concatenate([near[0][kernel], near[1][kernel]], axis=0)

        @pl.when(core == 0)
        def _():
            left[kernel] = own()

        @pl.when(core == 1)
        def _():
            left[kernel] = other()

        total = product(left[kernel], steps[kernel, :, 0 : 3 * n])
        store(out, scale, 4, kernel, total)

        @pl.when(same)
        def _():
            store(out, scale, 7, kernel, product(other(), own()))

        @pl.when(packed)
        def _():
            mine, yours = product(own(), own()), product(other(), other())
            high = jnp.where(y == 0, mine, yours)
            low = jnp.where(y == 0, yours, mine)
            row = lax.broadcasted_iota(jnp.int32, (n, n), 0)
            col = lax.broadcasted_iota(jnp.int32, (n, n), 1)
            store(out, scale, 3, kernel, jnp.where(row <= col, high, low))
            diagonal = jnp.sum(jnp.where(row == col, low, 0.0), axis=0, keepdims=True)
            line = lax.broadcasted_iota(jnp.int32, (EXTRA, n), 0)
            extra = out[3, 2 * n : 2 * n + EXTRA].astype(jnp.float32)
            extra = jnp.where(line == kernel, diagonal * scale, extra)
            out[3, 2 * n : 2 * n + EXTRA] = extra.astype(jnp.bfloat16)


def middle_kernel(place, scales, first, second, far, left, _, __, out, steps, total):
    scale = scales[place[3]]
    _, same, turned = cases(place)
    n = out.shape[-1]
    rows = far.shape[1]
    for kernel in range(2):
        last = jnp.concatenate([first[kernel], second[kernel]], axis=0)

        @pl.when(jnp.logical_not(same))
        def _():
            store(out, scale, 7, kernel, product(left[kernel], last))

        @pl.when(turned)
        def _():
            steps[kernel, :, 3 * n :] = left[kernel]

        @pl.when(jnp.logical_not(turned))
        def _():
            steps[kernel, :, 3 * n :] = last

        total[kernel] = product(far[kernel], steps[kernel, rows:])


def late_kernel(place, scales, far, steps, part, _, out):
    scale = scales[place[3]]
    packed, _, _ = cases(place)
    n = out.shape[-1]
    rows = far.shape[1]
    for kernel in range(2):
        total = part[kernel] + product(far[kernel], steps[kernel, 0:rows])
        store(out, scale, 0, kernel, total[:, : 3 * n])

        @pl.when(jnp.logical_not(packed))
        def _():
            store(out, scale, 3, kernel, total[:, 3 * n :])


def place_kernel(total_draws, todo, a, b, feature, gradient):
    n = feature.shape[0]
    row = lax.broadcasted_iota(jnp.int32, (n, n), 0)
    col = lax.broadcasted_iota(jnp.int32, (n, n), 1)
    for kernel, out in enumerate((feature, gradient)):
        block, line = pl.ds(kernel * n, n), pl.ds(2 * n + kernel, 1)
        for half in range(2):
            second, mode = todo[2 * half] == 1, todo[2 * half + 1]
            got = jnp.where(second, b[block, :], a[block, :])
            extra = jnp.where(second, b[line, :], a[line, :])
            turned = got.T
            lower = row > col
            plain = (mode == 0) | ((mode == 2) & (row <= col)) | ((mode == 3) & lower)
            value = jnp.where(plain, got, turned)
            value = jnp.where((mode == 3) & (row == col), extra, value)
            out[:, half * n : (half + 1) * n] = value / total_draws


def on_device(field, backward):
    draws, n = field.shape
    total_draws = draws * 16
    both = pl.pallas_call(
        features_kernel,
        out_shape=jax.ShapeDtypeStruct((2, draws, n), jnp.bfloat16),
        in_specs=[pl.BlockSpec(memory_space=pltpu.HBM)] * 2,
        out_specs=VMEM,
        scratch_shapes=[
            pltpu.VMEM((draws, n), jnp.bfloat16),
            pltpu.VMEM((draws, n), jnp.bfloat16),
            pltpu.SemaphoreType.DMA((2, PIECES)),
        ],
        compiler_params=pltpu.CompilerParams(vmem_limit_bytes=60 * 1024 * 1024),
    )(field, backward)

    step, first_step = [], []
    for c in range(2):
        for z in range(16):
            step.append((c * 16 + z, c * 16 + (z + 1 - 2 * c) % 16))
            first_step.append((c * 16 + z, (1 - c) * 16 + (z + 2 * c - 1) % 16))
    place = jnp.stack([lax.axis_index(a) for a in ("c", "yl", "z", ("yh", "x"))])
    scales = np.exp2(np.arange(8) / 8).astype(np.float32)
    shape = jax.ShapeDtypeStruct((8, 2 * n + EXTRA, n), jnp.bfloat16)
    left_shape = jax.ShapeDtypeStruct((2, 2 * draws, n), jnp.bfloat16)
    steps_shape = jax.ShapeDtypeStruct((2, 2 * draws, 4 * n), jnp.bfloat16)
    total_shape = jax.ShapeDtypeStruct((2, n, 4 * n), jnp.float32)

    def call(kernel, out_shape, *args, aliases={}, flops=1):
        return pl.pallas_call(
            kernel,
            out_shape=out_shape,
            in_specs=[SMEM, SMEM] + [VMEM] * len(args),
            out_specs=jax.tree.map(lambda _: VMEM, out_shape),
            input_output_aliases=aliases,
            compiler_params=PARAMS,
            cost_estimate=pl.CostEstimate(
                flops=flops * 8 * n * n * draws,
                bytes_accessed=28 * n * draws,
                transcendentals=0,
            ),
        )(place, jnp.asarray(scales), *args)

    chains = [
        lax.ppermute(both, ("c", "z"), step),
        lax.ppermute(both, ("c", "z"), first_step),
    ]
    walk = [[], []]
    for j in range(4):
        if j:
            chains = [lax.ppermute(chain, ("c", "z"), step) for chain in chains]
        if j == 0:
            other = lax.ppermute(both, "c", [(0, 1), (1, 0)])
            other, chains[1] = lax.optimization_barrier((other, chains[1]))
            own, chains[1] = lax.optimization_barrier((both, chains[1]))
            near = [lax.ppermute(own, ("c", "yl"), [(2, 3), (3, 2)])]
        if j == 1:
            own, chains[1] = lax.optimization_barrier((both, chains[1]))
            near.append(lax.ppermute(own, ("c", "yl"), [(0, 3), (1, 2)]))
            near[0], chains[1] = lax.optimization_barrier((near[0], chains[1]))
        if j == 2:
            near[1], chains[1] = lax.optimization_barrier((near[1], chains[1]))
        if j == 3:
            partial, left, steps = call(
                early_kernel,
                (shape, left_shape, steps_shape),
                *(both, *walk[0], other, *walk[1], *near),
                flops=4,
            )
            partial, chains[1] = lax.optimization_barrier((partial, chains[1]))
        for chain, blocks in zip(chains, walk):
            blocks.append(chain)
    cross = [(0, 2), (1, 3), (2, 1), (3, 0)]
    far = [lax.ppermute(chain, ("c", "yl"), cross) for chain in chains]

    partial, steps, total = call(
        middle_kernel,
        (shape, steps_shape, total_shape),
        *(*chains, far[0], left, partial, steps),
        aliases={6: 0, 7: 1},
        flops=3,
    )
    partial = call(late_kernel, shape, far[1], steps, total, partial, aliases={5: 0}, flops=2)
    partial = lax.all_to_all(partial, ("yh", "x"), 0, 0, tiled=True)
    block = jnp.sum(partial.astype(jnp.float32) / scales[:, None, None], axis=0)
    block = block[: 2 * n + 8]

    perms, table = routes()
    a = lax.ppermute(block, AXES, perms[0])
    b = lax.ppermute(block, AXES, perms[1])
    todo = lax.dynamic_index_in_dim(
        jnp.asarray(table), lax.axis_index(AXES), 0, keepdims=False
    )
    out = jax.ShapeDtypeStruct((n, 2 * n), jnp.float32)
    return pl.pallas_call(
        functools.partial(place_kernel, total_draws),
        out_shape=(out, out),
        in_specs=[SMEM, VMEM, VMEM],
        out_specs=(VMEM, VMEM),
        compiler_params=PARAMS,
    )(todo, a, b)


def solution(mesh):
    grid = Mesh(mesh.devices.reshape(SIZES), AXES)
    return jax.shard_map(
        on_device,
        mesh=grid,
        in_specs=(P(("yh", "x", "c"), ("yl", "z")),) * 2,
        out_specs=(P(("yl", "z"), ("yh", "x", "c")),) * 2,
        check_vma=False,
    )
```

```python
import functools

import jax
import jax.numpy as jnp
import numpy as np
from jax import lax
from jax.experimental import pallas as pl
from jax.experimental.pallas import tpu as pltpu
from jax.sharding import Mesh, PartitionSpec as P

AXES = ("yh", "x", "c", "yl", "z")
SIZES = (2, 4, 2, 2, 16)
PIECES = 4
SCALES = [float(np.float32(2 ** (i / 8))) for i in range(8)]
TOP = 14.0
EXTRA = 16
VMEM = pl.BlockSpec(memory_space=pltpu.VMEM)
SMEM = pl.BlockSpec(memory_space=pltpu.SMEM)
PARAMS = pltpu.CompilerParams(vmem_limit_bytes=40 * 1024 * 1024)


def device_index(yh, x, c, yl, z):
    return (((yh * 4 + x) * 2 + c) * 2 + yl) * 16 + z


def home(row_y, row_z, col_y, col_z):
    return device_index(col_y, col_z // 4, col_z % 4 // 2, row_y, row_z), col_z % 2


def homes(yh, x, c, yl, z):
    slot = yh * 4 + x
    if c == 0:
        left = (yl, z) if slot > 3 else (1 - yl, z + 4)
        right = (yl, z - slot % 4 - 1)
        if slot == 3 and yl == 1:
            right = (yl, z)
    else:
        left = (1 - yl, z) if slot > 3 else (yl, z - 4)
        right = (yl, z + slot % 4 + 1)
        if slot == 3 and (z < 8) != (yl == 0):
            return [home(0, z, 0, z) + (2,), home(1, z, 1, z) + (3,)]
        if slot == 7 and yl == 0:
            right = (yl, z)
    left, right = (left[0], left[1] % 16), (right[0], right[1] % 16)
    return [home(*left, *right) + (0,), home(*right, *left) + (1,)]


def routes():
    edges = []
    for place in np.ndindex(*SIZES):
        for to, half, mode in homes(*place):
            edges.append((device_index(*place), to, half, mode))
    into = [[] for _ in range(512)]
    for e, edge in enumerate(edges):
        into[edge[1]].append(e)
    turn = [-1] * len(edges)
    for first in range(len(edges)):
        e = first
        while turn[e] < 0:
            turn[e] = 0
            pair = into[edges[e][1]]
            other = pair[0] + pair[1] - e
            turn[other] = 1
            e = other ^ 1
    perms = [[], []]
    table = np.zeros((512, 4), np.int32)
    for e, (source, to, half, mode) in enumerate(edges):
        perms[turn[e]].append((source, to))
        table[to, 2 * half] = turn[e]
        table[to, 2 * half + 1] = mode
    return perms, table


def features_kernel(field, backward, both, f, b, sems):
    rows = field.shape[0] // PIECES
    copies = []
    for piece in range(PIECES):
        part = pl.ds(piece * rows, rows)
        copies.append(
            [
                pltpu.make_async_copy(src.at[part], dst.at[part], sems.at[i, piece])
                for i, (src, dst) in enumerate(((field, f), (backward, b)))
            ]
        )
        for copy in copies[-1]:
            copy.start()
    for piece in range(PIECES):
        part = pl.ds(piece * rows, rows)
        for copy in copies[piece]:
            copy.wait()
        wide = jnp.tanh(f[part, :].astype(jnp.float32))
        gated = (1.0 - wide * wide) * b[part, :].astype(jnp.float32)
        both[0, part, :] = wide.astype(jnp.bfloat16)
        both[1, part, :] = gated.astype(jnp.bfloat16)


def product(left, right):
    return lax.dot_general(
        left, right, (((0,), (0,)), ((), ())), preferred_element_type=jnp.float32
    )


def scale_of(place):
    scale = jnp.float32(SCALES[0])
    for i in range(1, len(SCALES)):
        scale = jnp.where(place[3] == i, SCALES[i], scale)
    return scale


def store(out, scale, slot, kernel, total):
    n = out.shape[-1]
    for j in range(total.shape[1] // n):
        block = total[:, j * n : (j + 1) * n] * scale
        out[slot + j, kernel * n : (kernel + 1) * n] = block.astype(jnp.bfloat16)


def cases(place):
    core, y, z = place[0], place[1], place[2]
    return (core == 1) & ((z < 8) != (y == 0)), (core == 1) & (y == 0), (core == 0) & (y == 1)


def early_kernel(place, *refs):
    first, second, near, (out, left, steps) = refs[0:4], refs[4:8], refs[8:10], refs[10:]
    core, y, scale = place[0], place[1], scale_of(place)
    packed, same, _ = cases(place)
    n = out.shape[-1]
    rows = near[0].shape[1]
    for slot in range(8):
        out[slot, 2 * n : 2 * n + EXTRA] = jnp.zeros((EXTRA, n), jnp.bfloat16)
    for kernel in range(2):
        for i, chain in enumerate((first, second)):
            part = pl.ds(i * rows, rows)
            for j in range(3):
                steps[kernel, part, j * n : (j + 1) * n] = chain[j + 1][kernel]

        def own(kernel=kernel):
            return jnp.concatenate([first[0][kernel], second[0][kernel]], axis=0)

        def other(kernel=kernel):
            return jnp.concatenate([near[0][kernel], near[1][kernel]], axis=0)

        @pl.when(core == 0)
        def _():
            left[kernel] = own()

        @pl.when(core == 1)
        def _():
            left[kernel] = other()

        total = product(left[kernel], steps[kernel, :, 0 : 3 * n])
        store(out, scale, 4, kernel, total)

        @pl.when(same)
        def _():
            store(out, scale, 7, kernel, product(other(), own()))

        @pl.when(packed)
        def _():
            mine, yours = product(own(), own()), product(other(), other())
            high = jnp.where(y == 0, mine, yours)
            low = jnp.where(y == 0, yours, mine)
            row = lax.broadcasted_iota(jnp.int32, (n, n), 0)
            col = lax.broadcasted_iota(jnp.int32, (n, n), 1)
            store(out, scale, 3, kernel, jnp.where(row <= col, high, low))
            diagonal = jnp.sum(jnp.where(row == col, low, 0.0), axis=0, keepdims=True)
            line = lax.broadcasted_iota(jnp.int32, (EXTRA, n), 0)
            extra = out[3, 2 * n : 2 * n + EXTRA].astype(jnp.float32)
            extra = jnp.where(line == kernel, diagonal * scale, extra)
            out[3, 2 * n : 2 * n + EXTRA] = extra.astype(jnp.bfloat16)


def middle_kernel(place, first, second, far, left, _, __, out, steps, total):
    scale = scale_of(place)
    _, same, turned = cases(place)
    n = out.shape[-1]
    rows = far.shape[1]
    for kernel in range(2):
        last = jnp.concatenate([first[kernel], second[kernel]], axis=0)

        @pl.when(jnp.logical_not(same))
        def _():
            store(out, scale, 7, kernel, product(left[kernel], last))

        @pl.when(turned)
        def _():
            steps[kernel, :, 3 * n :] = left[kernel]

        @pl.when(jnp.logical_not(turned))
        def _():
            steps[kernel, :, 3 * n :] = last

        total[kernel] = product(far[kernel], steps[kernel, rows:])


def late_kernel(place, far, steps, part, partial, out):
    out[...] = partial[...]
    scale = scale_of(place)
    packed, _, _ = cases(place)
    n = out.shape[-1]
    rows = far.shape[1]
    for kernel in range(2):
        total = part[kernel] + product(far[kernel], steps[kernel, 0:rows])
        store(out, scale, 0, kernel, total[:, : 3 * n])

        @pl.when(jnp.logical_not(packed))
        def _():
            store(out, scale, 3, kernel, total[:, 3 * n :])


def sum_kernel(parts, out):
    n = out.shape[-1]
    total = sum(
        parts[i].astype(jnp.float32) * (1 / scale) for i, scale in enumerate(SCALES)
    )
    line = lax.broadcasted_iota(jnp.int32, (8, n), 0)
    extra = total[2 * n : 2 * n + 8]
    for kernel in range(2):
        block = total[kernel * n : (kernel + 1) * n]
        diagonal = total[2 * n + kernel : 2 * n + kernel + 1]
        most = jnp.maximum(
            jnp.max(jnp.abs(block), axis=0, keepdims=True), jnp.abs(diagonal)
        )
        power = jnp.ceil(jnp.log2(jnp.maximum(most, 1e-30)))
        factor = jnp.exp2(TOP - power)
        out[kernel * n : (kernel + 1) * n] = block * factor
        extra = jnp.where(line == kernel, diagonal * factor, extra)
        extra = jnp.where(line == 2 + kernel, power, extra)
    out[2 * n :] = extra


def place_kernel(total_draws, todo, a, b, feature, gradient):
    n = feature.shape[0]
    row = lax.broadcasted_iota(jnp.int32, (n, n), 0)
    col = lax.broadcasted_iota(jnp.int32, (n, n), 1)
    for kernel, out in enumerate((feature, gradient)):
        block, line = pl.ds(kernel * n, n), pl.ds(2 * n + kernel, 1)
        power = pl.ds(2 * n + 2 + kernel, 1)
        for half in range(2):
            second, mode = todo[2 * half] == 1, todo[2 * half + 1]
            factor = jnp.exp2(jnp.where(second, b[power, :], a[power, :]) - TOP)
            got = jnp.where(second, b[block, :], a[block, :]) * factor
            extra = jnp.where(second, b[line, :], a[line, :]) * factor
            turned = got.T
            lower = row > col
            plain = (mode == 0) | ((mode == 2) & (row <= col)) | ((mode == 3) & lower)
            value = jnp.where(plain, got, turned)
            value = jnp.where((mode == 3) & (row == col), extra, value)
            out[:, half * n : (half + 1) * n] = value / total_draws


def on_device(field, backward):
    draws, n = field.shape
    total_draws = draws * 16
    both = pl.pallas_call(
        features_kernel,
        out_shape=jax.ShapeDtypeStruct((2, draws, n), jnp.bfloat16),
        in_specs=[pl.BlockSpec(memory_space=pltpu.HBM)] * 2,
        out_specs=VMEM,
        scratch_shapes=[
            pltpu.VMEM((draws, n), jnp.bfloat16),
            pltpu.VMEM((draws, n), jnp.bfloat16),
            pltpu.SemaphoreType.DMA((2, PIECES)),
        ],
        compiler_params=pltpu.CompilerParams(vmem_limit_bytes=60 * 1024 * 1024),
    )(field, backward)

    step, first_step = [], []
    for c in range(2):
        for z in range(16):
            step.append((c * 16 + z, c * 16 + (z + 1 - 2 * c) % 16))
            first_step.append((c * 16 + z, (1 - c) * 16 + (z + 2 * c - 1) % 16))
    place = jnp.stack([lax.axis_index(a) for a in ("c", "yl", "z", ("yh", "x"))])
    shape = jax.ShapeDtypeStruct((8, 2 * n + EXTRA, n), jnp.bfloat16)
    left_shape = jax.ShapeDtypeStruct((2, 2 * draws, n), jnp.bfloat16)
    steps_shape = jax.ShapeDtypeStruct((2, 2 * draws, 4 * n), jnp.bfloat16)
    total_shape = jax.ShapeDtypeStruct((2, n, 4 * n), jnp.float32)

    def call(kernel, out_shape, *args, aliases={}, flops=1):
        return pl.pallas_call(
            kernel,
            out_shape=out_shape,
            in_specs=[SMEM] + [VMEM] * len(args),
            out_specs=jax.tree.map(lambda _: VMEM, out_shape),
            input_output_aliases=aliases,
            compiler_params=PARAMS,
            cost_estimate=pl.CostEstimate(
                flops=flops * 8 * n * n * draws,
                bytes_accessed=28 * n * draws,
                transcendentals=0,
            ),
        )(place, *args)

    chains = [
        lax.ppermute(both, ("c", "z"), step),
        lax.ppermute(both, ("c", "z"), first_step),
    ]
    walk = [[], []]
    other = lax.ppermute(both, "c", [(0, 1), (1, 0)])
    partners = (("c", "yl"), [(2, 3), (3, 2)])
    for j in range(4):
        if j:
            chains = [lax.ppermute(chain, ("c", "z"), step) for chain in chains]
        if j == 0:
            own, chains[1] = lax.optimization_barrier((both, chains[1]))
            near = [lax.ppermute(own, *partners)]
            other, chains[0] = lax.optimization_barrier((other, chains[0]))
        if j == 1:
            again, chains[1] = lax.optimization_barrier((other, chains[1]))
            near.append(lax.ppermute(again, *partners))
            near[0], chains[1] = lax.optimization_barrier((near[0], chains[1]))
        if j == 3:
            partial, left, steps = call(
                early_kernel,
                (shape, left_shape, steps_shape),
                *(both, *walk[0], other, *walk[1], *near),
                flops=4,
            )
            partial, chains[1] = lax.optimization_barrier((partial, chains[1]))
        for chain, blocks in zip(chains, walk):
            blocks.append(chain)
    cross = [(0, 2), (1, 3), (2, 1), (3, 0)]
    far = [lax.ppermute(chain, ("c", "yl"), cross) for chain in chains]

    partial, steps, total = call(
        middle_kernel,
        (shape, steps_shape, total_shape),
        *(*chains, far[0], left, partial, steps),
        aliases={5: 0, 6: 1},
        flops=3,
    )
    partial = call(late_kernel, shape, far[1], steps, total, partial, flops=2)
    partial = lax.all_to_all(partial, ("yh", "x"), 0, 0, tiled=True)
    block = pl.pallas_call(
        sum_kernel,
        out_shape=jax.ShapeDtypeStruct((2 * n + 8, n), jnp.float32),
        in_specs=[VMEM],
        out_specs=VMEM,
        compiler_params=PARAMS,
    )(partial).astype(jnp.float16)

    perms, table = routes()
    a, b = [lax.ppermute(block, AXES, p).astype(jnp.float32) for p in perms]
    todo = lax.dynamic_index_in_dim(
        jnp.asarray(table), lax.axis_index(AXES), 0, keepdims=False
    )
    out = jax.ShapeDtypeStruct((n, 2 * n), jnp.float32)
    return pl.pallas_call(
        functools.partial(place_kernel, total_draws),
        out_shape=(out, out),
        in_specs=[SMEM, VMEM, VMEM],
        out_specs=(VMEM, VMEM),
        compiler_params=PARAMS,
    )(todo, a, b)


def solution(mesh):
    grid = Mesh(mesh.devices.reshape(SIZES), AXES)
    return jax.shard_map(
        on_device,
        mesh=grid,
        in_specs=(P(("yh", "x", "c"), ("yl", "z")),) * 2,
        out_specs=(P(("yl", "z"), ("yh", "x", "c")),) * 2,
        check_vma=False,
    )
```

```python
import functools

import jax
import jax.numpy as jnp
import numpy as np
from jax import lax
from jax.experimental import pallas as pl
from jax.experimental.pallas import tpu as pltpu
from jax.sharding import Mesh, PartitionSpec as P

AXES = ("yh", "x", "c", "yl", "z")
SIZES = (2, 4, 2, 2, 16)
PIECES = 4
SCALES = [float(np.float32(2 ** (i / 8))) for i in range(8)]
TOP = 14.0
EXTRA = 16
VMEM = pl.BlockSpec(memory_space=pltpu.VMEM)
SMEM = pl.BlockSpec(memory_space=pltpu.SMEM)
PARAMS = pltpu.CompilerParams(vmem_limit_bytes=40 * 1024 * 1024)


def device_index(yh, x, c, yl, z):
    return (((yh * 4 + x) * 2 + c) * 2 + yl) * 16 + z


def home(row_y, row_z, col_y, col_z):
    return device_index(col_y, col_z // 4, col_z % 4 // 2, row_y, row_z), col_z % 2


def rank_or_slot(i, core, y):
    return i ^ (4 * (y ^ (1 - core)))


def homes(yh, x, c, yl, z):
    slot = rank_or_slot(yh * 4 + x, c, yl)
    if c == 0:
        left = (yl, z) if slot > 3 else (1 - yl, z + 4)
        right = (yl, z - slot % 4 - 1)
        if slot == 3 and yl == 1:
            right = (yl, z)
    else:
        left = (1 - yl, z) if slot > 3 else (yl, z - 4)
        right = (yl, z + slot % 4 + 1)
        if slot == 3 and (z < 8) != (yl == 0):
            return [home(0, z, 0, z) + (2,), home(1, z, 1, z) + (3,)]
        if slot == 7 and yl == 0:
            right = (yl, z)
    left, right = (left[0], left[1] % 16), (right[0], right[1] % 16)
    return [home(*left, *right) + (0,), home(*right, *left) + (1,)]


def routes():
    edges = []
    for place in np.ndindex(*SIZES):
        for to, half, mode in homes(*place):
            edges.append((device_index(*place), to, half, mode))
    into = [[] for _ in range(512)]
    for e, edge in enumerate(edges):
        into[edge[1]].append(e)
    turn = [-1] * len(edges)
    for first in range(len(edges)):
        e = first
        while turn[e] < 0:
            turn[e] = 0
            pair = into[edges[e][1]]
            other = pair[0] + pair[1] - e
            turn[other] = 1
            e = other ^ 1
    perms = [[], []]
    table = np.zeros((512, 4), np.int32)
    for e, (source, to, half, mode) in enumerate(edges):
        perms[turn[e]].append((source, to))
        table[to, 2 * half] = turn[e]
        table[to, 2 * half + 1] = mode
    return perms, table


def features_kernel(field, backward, both, f, b, sems):
    rows = field.shape[0] // PIECES
    copies = []
    for piece in range(PIECES):
        part = pl.ds(piece * rows, rows)
        copies.append(
            [
                pltpu.make_async_copy(src.at[part], dst.at[part], sems.at[i, piece])
                for i, (src, dst) in enumerate(((field, f), (backward, b)))
            ]
        )
        for copy in copies[-1]:
            copy.start()
    for piece in range(PIECES):
        part = pl.ds(piece * rows, rows)
        for copy in copies[piece]:
            copy.wait()
        wide = jnp.tanh(f[part, :].astype(jnp.float32))
        gated = (1.0 - wide * wide) * b[part, :].astype(jnp.float32)
        both[0, part, :] = wide.astype(jnp.bfloat16)
        both[1, part, :] = gated.astype(jnp.bfloat16)


def product(left, right):
    return lax.dot_general(
        left, right, (((0,), (0,)), ((), ())), preferred_element_type=jnp.float32
    )


def scale_of(place):
    scale = jnp.float32(SCALES[0])
    for i in range(1, len(SCALES)):
        scale = jnp.where(place[3] == i, SCALES[i], scale)
    return scale


def store(out, place, slot, kernel, total):
    n, scale = out.shape[-1], scale_of(place)
    for j in range(total.shape[1] // n):
        block = total[:, j * n : (j + 1) * n] * scale
        to = rank_or_slot(slot + j, place[0], place[1])
        out[to, kernel * n : (kernel + 1) * n] = block.astype(jnp.bfloat16)


def cases(place):
    core, y, z = place[0], place[1], place[2]
    return (core == 1) & ((z < 8) != (y == 0)), (core == 1) & (y == 0), (core == 0) & (y == 1)


def early_kernel(place, *refs):
    first, second, near, (out, left, steps) = refs[0:4], refs[4:8], refs[8:10], refs[10:]
    core, y, scale = place[0], place[1], scale_of(place)
    packed, same, _ = cases(place)
    n = out.shape[-1]
    rows = near[0].shape[1]
    for slot in range(8):
        out[slot, 2 * n : 2 * n + EXTRA] = jnp.zeros((EXTRA, n), jnp.bfloat16)
    for kernel in range(2):
        for i, chain in enumerate((first, second)):
            part = pl.ds(i * rows, rows)
            for j in range(3):
                steps[kernel, part, j * n : (j + 1) * n] = chain[j + 1][kernel]

        def own(kernel=kernel):
            return jnp.concatenate([first[0][kernel], second[0][kernel]], axis=0)

        def other(kernel=kernel):
            return jnp.concatenate([near[0][kernel], near[1][kernel]], axis=0)

        @pl.when(core == 0)
        def _():
            left[kernel] = own()

        @pl.when(core == 1)
        def _():
            left[kernel] = other()

        total = product(left[kernel], steps[kernel, :, 0 : 3 * n])
        store(out, place, 4, kernel, total)

        @pl.when(same)
        def _():
            store(out, place, 7, kernel, product(other(), own()))

        @pl.when(packed)
        def _():
            mine, yours = product(own(), own()), product(other(), other())
            high = jnp.where(y == 0, mine, yours)
            low = jnp.where(y == 0, yours, mine)
            row = lax.broadcasted_iota(jnp.int32, (n, n), 0)
            col = lax.broadcasted_iota(jnp.int32, (n, n), 1)
            store(out, place, 3, kernel, jnp.where(row <= col, high, low))
            diagonal = jnp.sum(jnp.where(row == col, low, 0.0), axis=0, keepdims=True)
            line = lax.broadcasted_iota(jnp.int32, (EXTRA, n), 0)
            to = rank_or_slot(3, core, y)
            extra = out[to, 2 * n : 2 * n + EXTRA].astype(jnp.float32)
            extra = jnp.where(line == kernel, diagonal * scale, extra)
            out[to, 2 * n : 2 * n + EXTRA] = extra.astype(jnp.bfloat16)


def middle_kernel(place, first, second, far, left, _, __, out, steps, total):
    _, same, turned = cases(place)
    n = out.shape[-1]
    rows = far.shape[1]
    for kernel in range(2):
        last = jnp.concatenate([first[kernel], second[kernel]], axis=0)

        @pl.when(jnp.logical_not(same))
        def _():
            store(out, place, 7, kernel, product(left[kernel], last))

        @pl.when(turned)
        def _():
            steps[kernel, :, 3 * n :] = left[kernel]

        @pl.when(jnp.logical_not(turned))
        def _():
            steps[kernel, :, 3 * n :] = last

        total[kernel] = product(far[kernel], steps[kernel, rows:])


def late_kernel(place, far, steps, part, _, out):
    packed, _, _ = cases(place)
    n = out.shape[-1]
    rows = far.shape[1]
    for kernel in range(2):
        total = part[kernel] + product(far[kernel], steps[kernel, 0:rows])
        store(out, place, 0, kernel, total[:, : 3 * n])

        @pl.when(jnp.logical_not(packed))
        def _():
            store(out, place, 3, kernel, total[:, 3 * n :])


def sum_kernel(parts, out):
    n = out.shape[-1]
    total = sum(
        parts[i].astype(jnp.float32) * (1 / scale) for i, scale in enumerate(SCALES)
    )
    line = lax.broadcasted_iota(jnp.int32, (8, n), 0)
    extra = total[2 * n : 2 * n + 8]
    for kernel in range(2):
        block = total[kernel * n : (kernel + 1) * n]
        diagonal = total[2 * n + kernel : 2 * n + kernel + 1]
        most = jnp.maximum(
            jnp.max(jnp.abs(block), axis=0, keepdims=True), jnp.abs(diagonal)
        )
        power = jnp.ceil(jnp.log2(jnp.maximum(most, 1e-30)))
        factor = jnp.exp2(TOP - power)
        out[kernel * n : (kernel + 1) * n] = block * factor
        extra = jnp.where(line == kernel, diagonal * factor, extra)
        extra = jnp.where(line == 2 + kernel, power, extra)
    out[2 * n :] = extra


def place_kernel(total_draws, place, todo, a, b, feature, gradient):
    n = feature.shape[0]
    row = lax.broadcasted_iota(jnp.int32, (n, n), 0)
    col = lax.broadcasted_iota(jnp.int32, (n, n), 1)
    code = todo[device_index(*[place[i] for i in range(5)])]
    for kernel, out in enumerate((feature, gradient)):
        block, line = pl.ds(kernel * n, n), pl.ds(2 * n + kernel, 1)
        power = pl.ds(2 * n + 2 + kernel, 1)
        for half in range(2):
            second, mode = code // 8**half % 2 == 1, code // 8**half // 2 % 4
            factor = jnp.exp2(jnp.where(second, b[power, :], a[power, :]) - TOP)
            got = jnp.where(second, b[block, :], a[block, :]) * factor
            extra = jnp.where(second, b[line, :], a[line, :]) * factor
            turned = got.T
            lower = row > col
            plain = (mode == 0) | ((mode == 2) & (row <= col)) | ((mode == 3) & lower)
            value = jnp.where(plain, got, turned)
            value = jnp.where((mode == 3) & (row == col), extra, value)
            out[:, half * n : (half + 1) * n] = value / total_draws


def on_device(field, backward):
    draws, n = field.shape
    total_draws = draws * 16
    both = pl.pallas_call(
        features_kernel,
        out_shape=jax.ShapeDtypeStruct((2, draws, n), jnp.bfloat16),
        in_specs=[pl.BlockSpec(memory_space=pltpu.HBM)] * 2,
        out_specs=VMEM,
        scratch_shapes=[
            pltpu.VMEM((draws, n), jnp.bfloat16),
            pltpu.VMEM((draws, n), jnp.bfloat16),
            pltpu.SemaphoreType.DMA((2, PIECES)),
        ],
        compiler_params=pltpu.CompilerParams(vmem_limit_bytes=60 * 1024 * 1024),
    )(field, backward)

    step, first_step = [], []
    for c in range(2):
        for z in range(16):
            step.append((c * 16 + z, c * 16 + (z + 1 - 2 * c) % 16))
            first_step.append((c * 16 + z, (1 - c) * 16 + (z + 2 * c - 1) % 16))
    place = jnp.stack([lax.axis_index(a) for a in ("c", "yl", "z", ("yh", "x"))])
    shape = jax.ShapeDtypeStruct((8, 2 * n + EXTRA, n), jnp.bfloat16)
    left_shape = jax.ShapeDtypeStruct((2, 2 * draws, n), jnp.bfloat16)
    steps_shape = jax.ShapeDtypeStruct((2, 2 * draws, 4 * n), jnp.bfloat16)
    total_shape = jax.ShapeDtypeStruct((2, n, 4 * n), jnp.float32)

    def call(kernel, out_shape, *args, aliases={}, flops=1):
        return pl.pallas_call(
            kernel,
            out_shape=out_shape,
            in_specs=[SMEM] + [VMEM] * len(args),
            out_specs=jax.tree.map(lambda _: VMEM, out_shape),
            input_output_aliases=aliases,
            compiler_params=PARAMS,
            cost_estimate=pl.CostEstimate(
                flops=flops * 8 * n * n * draws,
                bytes_accessed=28 * n * draws,
                transcendentals=0,
            ),
        )(place, *args)

    chains = [
        lax.ppermute(both, ("c", "z"), step),
        lax.ppermute(both, ("c", "z"), first_step),
    ]
    walk = [[], []]
    other = lax.ppermute(both, "c", [(0, 1), (1, 0)])
    partners = (("c", "yl"), [(2, 3), (3, 2)])
    for j in range(4):
        if j:
            chains = [lax.ppermute(chain, ("c", "z"), step) for chain in chains]
        if j == 0:
            own, chains[1] = lax.optimization_barrier((both, chains[1]))
            near = [lax.ppermute(own, *partners)]
            other, chains[0] = lax.optimization_barrier((other, chains[0]))
        if j == 1:
            again, chains[1] = lax.optimization_barrier((other, chains[1]))
            near.append(lax.ppermute(again, *partners))
            near[0], chains[1] = lax.optimization_barrier((near[0], chains[1]))
        if j == 3:
            partial, left, steps = call(
                early_kernel,
                (shape, left_shape, steps_shape),
                *(both, *walk[0], other, *walk[1], *near),
                flops=4,
            )
            partial, chains[1] = lax.optimization_barrier((partial, chains[1]))
        for chain, blocks in zip(chains, walk):
            blocks.append(chain)
    cross = [(0, 2), (1, 3), (2, 1), (3, 0)]
    far = [lax.ppermute(chain, ("c", "yl"), cross) for chain in chains]

    partial, steps, total = call(
        middle_kernel,
        (shape, steps_shape, total_shape),
        *(*chains, far[0], left, partial, steps),
        aliases={5: 0, 6: 1},
        flops=3,
    )
    perms, table = routes()
    partial = call(late_kernel, shape, far[1], steps, total, partial, aliases={4: 0}, flops=2)
    partial = lax.all_to_all(partial, ("yh", "x"), 0, 0, tiled=True)
    block = pl.pallas_call(
        sum_kernel,
        out_shape=jax.ShapeDtypeStruct((2 * n + 8, n), jnp.float32),
        in_specs=[VMEM],
        out_specs=VMEM,
        compiler_params=PARAMS,
    )(partial).astype(jnp.float16)

    a, b = [lax.ppermute(block, AXES, p).astype(jnp.float32) for p in perms]
    codes = table[:, 0::2] + 2 * table[:, 1::2]
    todo = jnp.asarray(codes[:, 0] + 8 * codes[:, 1])
    where = jnp.stack([lax.axis_index(a) for a in AXES])
    out = jax.ShapeDtypeStruct((n, 2 * n), jnp.float32)
    return pl.pallas_call(
        functools.partial(place_kernel, total_draws),
        out_shape=(out, out),
        in_specs=[SMEM, SMEM, VMEM, VMEM],
        out_specs=(VMEM, VMEM),
        compiler_params=PARAMS,
    )(where, todo, a, b)


def solution(mesh):
    grid = Mesh(mesh.devices.reshape(SIZES), AXES)
    return jax.shard_map(
        on_device,
        mesh=grid,
        in_specs=(P(("yh", "x", "c"), ("yl", "z")),) * 2,
        out_specs=(P(("yl", "z"), ("yh", "x", "c")),) * 2,
        check_vma=False,
    )
```

```python
import functools

import jax
import jax.numpy as jnp
import numpy as np
from jax import lax
from jax.experimental import pallas as pl
from jax.experimental.pallas import tpu as pltpu
from jax.sharding import Mesh, PartitionSpec as P

AXES = ("yh", "x", "c", "yl", "z")
SIZES = (2, 4, 2, 2, 16)
PIECES = 4
SCALES = [float(np.float32(2 ** (i / 8))) for i in range(8)]
TOP = 14.0
EXTRA = 16
VMEM = pl.BlockSpec(memory_space=pltpu.VMEM)
SMEM = pl.BlockSpec(memory_space=pltpu.SMEM)
PARAMS = pltpu.CompilerParams(vmem_limit_bytes=40 * 1024 * 1024)


def device_index(yh, x, c, yl, z):
    return (((yh * 4 + x) * 2 + c) * 2 + yl) * 16 + z


def home(row_y, row_z, col_y, col_z):
    return device_index(col_y, col_z // 4, col_z % 4 // 2, row_y, row_z), col_z % 2


def rank_or_slot(i, core, y):
    return i ^ (4 * (y ^ (1 - core)))


def homes(yh, x, c, yl, z):
    slot = rank_or_slot(yh * 4 + x, c, yl)
    if c == 0:
        left = (yl, z) if slot > 3 else (1 - yl, z + 4)
        right = (yl, z - slot % 4 - 1)
        if slot == 3 and yl == 1:
            right = (yl, z)
    else:
        left = (1 - yl, z) if slot > 3 else (yl, z - 4)
        right = (yl, z + slot % 4 + 1)
        if slot == 3 and (z < 8) != (yl == 0):
            return [home(0, z, 0, z) + (2,), home(1, z, 1, z) + (3,)]
        if slot == 7 and yl == 0:
            right = (yl, z)
    left, right = (left[0], left[1] % 16), (right[0], right[1] % 16)
    return [home(*left, *right) + (0,), home(*right, *left) + (1,)]


def routes():
    edges = []
    for place in np.ndindex(*SIZES):
        for to, half, mode in homes(*place):
            edges.append((device_index(*place), to, half, mode))
    into = [[] for _ in range(512)]
    for e, edge in enumerate(edges):
        into[edge[1]].append(e)
    def hops(e):
        there = np.unravel_index(edges[e][0], SIZES), np.unravel_index(edges[e][1], SIZES)
        (h0, x0, _, l0, z0), (h1, x1, _, l1, z1) = there
        return sum(
            min((p - q) % n, (q - p) % n)
            for p, q, n in ((x0, x1, 4), (2 * h0 + l0, 2 * h1 + l1, 4), (z0, z1, 16))
        )

    turn = [-1] * len(edges)
    for first in range(len(edges)):
        e, ways = first, ([], [])
        while turn[e] < 0:
            turn[e] = 0
            pair = into[edges[e][1]]
            other = pair[0] + pair[1] - e
            turn[other] = 1
            ways[0].append(e)
            ways[1].append(other)
            e = other ^ 1
        costs = [sum(map(hops, way)) for way in ways]
        if ways[0] and costs[1] < costs[0]:
            for e in ways[0]:
                turn[e] = 1
            for e in ways[1]:
                turn[e] = 0
    perms = [[], []]
    table = np.zeros((512, 4), np.int32)
    for e, (source, to, half, mode) in enumerate(edges):
        perms[turn[e]].append((source, to))
        table[to, 2 * half] = turn[e]
        table[to, 2 * half + 1] = mode
    return perms, table


def features_kernel(field, backward, both, f, b, sems):
    rows = field.shape[0] // PIECES
    copies = []
    for piece in range(PIECES):
        part = pl.ds(piece * rows, rows)
        copies.append(
            [
                pltpu.make_async_copy(src.at[part], dst.at[part], sems.at[i, piece])
                for i, (src, dst) in enumerate(((field, f), (backward, b)))
            ]
        )
        for copy in copies[-1]:
            copy.start()
    for piece in range(PIECES):
        part = pl.ds(piece * rows, rows)
        for copy in copies[piece]:
            copy.wait()
        wide = jnp.tanh(f[part, :].astype(jnp.float32))
        gated = (1.0 - wide * wide) * b[part, :].astype(jnp.float32)
        both[0, part, :] = wide.astype(jnp.bfloat16)
        both[1, part, :] = gated.astype(jnp.bfloat16)


def product(left, right):
    return lax.dot_general(
        left, right, (((0,), (0,)), ((), ())), preferred_element_type=jnp.float32
    )


def scale_of(place):
    scale = jnp.float32(SCALES[0])
    for i in range(1, len(SCALES)):
        scale = jnp.where(place[3] == i, SCALES[i], scale)
    return scale


def store(out, place, slot, kernel, total):
    n, scale = out.shape[-1], scale_of(place)
    for j in range(total.shape[1] // n):
        block = total[:, j * n : (j + 1) * n] * scale
        to = rank_or_slot(slot + j, place[0], place[1])
        out[to, kernel * n : (kernel + 1) * n] = block.astype(jnp.bfloat16)


def cases(place):
    core, y, z = place[0], place[1], place[2]
    return (core == 1) & ((z < 8) != (y == 0)), (core == 1) & (y == 0), (core == 0) & (y == 1)


def early_kernel(place, *refs):
    first, second, near, (out, left, steps) = refs[0:4], refs[4:8], refs[8:10], refs[10:]
    core, y, scale = place[0], place[1], scale_of(place)
    packed, same, _ = cases(place)
    n = out.shape[-1]
    rows = near[0].shape[1]
    for slot in range(8):
        out[slot, 2 * n : 2 * n + EXTRA] = jnp.zeros((EXTRA, n), jnp.bfloat16)
    for kernel in range(2):
        for i, chain in enumerate((first, second)):
            part = pl.ds(i * rows, rows)
            for j in range(3):
                steps[kernel, part, j * n : (j + 1) * n] = chain[j + 1][kernel]

        def own(kernel=kernel):
            return jnp.concatenate([first[0][kernel], second[0][kernel]], axis=0)

        def other(kernel=kernel):
            return jnp.concatenate([near[0][kernel], near[1][kernel]], axis=0)

        @pl.when(core == 0)
        def _():
            left[kernel] = own()

        @pl.when(core == 1)
        def _():
            left[kernel] = other()

        total = product(left[kernel], steps[kernel, :, 0 : 3 * n])
        store(out, place, 4, kernel, total)

        @pl.when(same)
        def _():
            store(out, place, 7, kernel, product(other(), own()))

        @pl.when(packed)
        def _():
            mine, yours = product(own(), own()), product(other(), other())
            high = jnp.where(y == 0, mine, yours)
            low = jnp.where(y == 0, yours, mine)
            row = lax.broadcasted_iota(jnp.int32, (n, n), 0)
            col = lax.broadcasted_iota(jnp.int32, (n, n), 1)
            store(out, place, 3, kernel, jnp.where(row <= col, high, low))
            diagonal = jnp.sum(jnp.where(row == col, low, 0.0), axis=0, keepdims=True)
            line = lax.broadcasted_iota(jnp.int32, (EXTRA, n), 0)
            to = rank_or_slot(3, core, y)
            extra = out[to, 2 * n : 2 * n + EXTRA].astype(jnp.float32)
            extra = jnp.where(line == kernel, diagonal * scale, extra)
            out[to, 2 * n : 2 * n + EXTRA] = extra.astype(jnp.bfloat16)


def middle_kernel(place, first, second, far, left, _, __, out, steps, total):
    _, same, turned = cases(place)
    n = out.shape[-1]
    rows = far.shape[1]
    for kernel in range(2):
        last = jnp.concatenate([first[kernel], second[kernel]], axis=0)

        @pl.when(jnp.logical_not(same))
        def _():
            store(out, place, 7, kernel, product(left[kernel], last))

        @pl.when(turned)
        def _():
            steps[kernel, :, 3 * n :] = left[kernel]

        @pl.when(jnp.logical_not(turned))
        def _():
            steps[kernel, :, 3 * n :] = last

        total[kernel] = product(far[kernel], steps[kernel, rows:])


def late_kernel(place, far, steps, part, _, out):
    packed, _, _ = cases(place)
    n = out.shape[-1]
    rows = far.shape[1]
    for kernel in range(2):
        total = part[kernel] + product(far[kernel], steps[kernel, 0:rows])
        store(out, place, 0, kernel, total[:, : 3 * n])

        @pl.when(jnp.logical_not(packed))
        def _():
            store(out, place, 3, kernel, total[:, 3 * n :])


def sum_kernel(parts, out):
    n = out.shape[-1]
    total = sum(
        parts[i].astype(jnp.float32) * (1 / scale) for i, scale in enumerate(SCALES)
    )
    line = lax.broadcasted_iota(jnp.int32, (8, n), 0)
    extra = total[2 * n : 2 * n + 8]
    for kernel in range(2):
        block = total[kernel * n : (kernel + 1) * n]
        diagonal = total[2 * n + kernel : 2 * n + kernel + 1]
        most = jnp.maximum(
            jnp.max(jnp.abs(block), axis=0, keepdims=True), jnp.abs(diagonal)
        )
        power = jnp.ceil(jnp.log2(jnp.maximum(most, 1e-30)))
        factor = jnp.exp2(TOP - power)
        out[kernel * n : (kernel + 1) * n] = block * factor
        extra = jnp.where(line == kernel, diagonal * factor, extra)
        extra = jnp.where(line == 2 + kernel, power, extra)
    out[2 * n :] = extra


def place_kernel(total_draws, place, todo, a, b, feature, gradient):
    n = feature.shape[0]
    row = lax.broadcasted_iota(jnp.int32, (n, n), 0)
    col = lax.broadcasted_iota(jnp.int32, (n, n), 1)
    code = todo[device_index(*[place[i] for i in range(5)])]
    for kernel, out in enumerate((feature, gradient)):
        block, line = pl.ds(kernel * n, n), pl.ds(2 * n + kernel, 1)
        power = pl.ds(2 * n + 2 + kernel, 1)
        for half in range(2):
            second, mode = code // 8**half % 2 == 1, code // 8**half // 2 % 4
            factor = jnp.exp2(jnp.where(second, b[power, :], a[power, :]) - TOP)
            got = jnp.where(second, b[block, :], a[block, :]) * factor
            extra = jnp.where(second, b[line, :], a[line, :]) * factor
            turned = got.T
            lower = row > col
            plain = (mode == 0) | ((mode == 2) & (row <= col)) | ((mode == 3) & lower)
            value = jnp.where(plain, got, turned)
            value = jnp.where((mode == 3) & (row == col), extra, value)
            out[:, half * n : (half + 1) * n] = value / total_draws


def on_device(field, backward):
    draws, n = field.shape
    total_draws = draws * 16
    both = pl.pallas_call(
        features_kernel,
        out_shape=jax.ShapeDtypeStruct((2, draws, n), jnp.bfloat16),
        in_specs=[pl.BlockSpec(memory_space=pltpu.HBM)] * 2,
        out_specs=VMEM,
        scratch_shapes=[
            pltpu.VMEM((draws, n), jnp.bfloat16),
            pltpu.VMEM((draws, n), jnp.bfloat16),
            pltpu.SemaphoreType.DMA((2, PIECES)),
        ],
        compiler_params=pltpu.CompilerParams(vmem_limit_bytes=60 * 1024 * 1024),
    )(field, backward)

    step, first_step = [], []
    for c in range(2):
        for z in range(16):
            step.append((c * 16 + z, c * 16 + (z + 1 - 2 * c) % 16))
            first_step.append((c * 16 + z, (1 - c) * 16 + (z + 2 * c - 1) % 16))
    place = jnp.stack([lax.axis_index(a) for a in ("c", "yl", "z", ("yh", "x"))])
    shape = jax.ShapeDtypeStruct((8, 2 * n + EXTRA, n), jnp.bfloat16)
    left_shape = jax.ShapeDtypeStruct((2, 2 * draws, n), jnp.bfloat16)
    steps_shape = jax.ShapeDtypeStruct((2, 2 * draws, 4 * n), jnp.bfloat16)
    total_shape = jax.ShapeDtypeStruct((2, n, 4 * n), jnp.float32)

    def call(kernel, out_shape, *args, aliases={}, flops=1):
        return pl.pallas_call(
            kernel,
            out_shape=out_shape,
            in_specs=[SMEM] + [VMEM] * len(args),
            out_specs=jax.tree.map(lambda _: VMEM, out_shape),
            input_output_aliases=aliases,
            compiler_params=PARAMS,
            cost_estimate=pl.CostEstimate(
                flops=flops * 8 * n * n * draws,
                bytes_accessed=28 * n * draws,
                transcendentals=0,
            ),
        )(place, *args)

    chains = [
        lax.ppermute(both, ("c", "z"), step),
        lax.ppermute(both, ("c", "z"), first_step),
    ]
    walk = [[], []]
    other = lax.ppermute(both, "c", [(0, 1), (1, 0)])
    partners = (("c", "yl"), [(2, 3), (3, 2)])
    for j in range(4):
        if j:
            chains = [lax.ppermute(chain, ("c", "z"), step) for chain in chains]
        if j == 0:
            own, chains[1] = lax.optimization_barrier((both, chains[1]))
            near = [lax.ppermute(own, *partners)]
            other, chains[0] = lax.optimization_barrier((other, chains[0]))
        if j == 1:
            again, chains[1] = lax.optimization_barrier((other, chains[1]))
            near.append(lax.ppermute(again, *partners))
            near[0], chains[1] = lax.optimization_barrier((near[0], chains[1]))
        if j == 3:
            partial, left, steps = call(
                early_kernel,
                (shape, left_shape, steps_shape),
                *(both, *walk[0], other, *walk[1], *near),
                flops=4,
            )
            partial, chains[1] = lax.optimization_barrier((partial, chains[1]))
        for chain, blocks in zip(chains, walk):
            blocks.append(chain)
    cross = [(0, 2), (1, 3), (2, 1), (3, 0)]
    far = [lax.ppermute(chain, ("c", "yl"), cross) for chain in chains]

    partial, steps, total = call(
        middle_kernel,
        (shape, steps_shape, total_shape),
        *(*chains, far[0], left, partial, steps),
        aliases={5: 0, 6: 1},
        flops=3,
    )
    perms, table = routes()
    partial = call(late_kernel, shape, far[1], steps, total, partial, aliases={4: 0}, flops=2)
    partial = lax.all_to_all(partial, ("yh", "x"), 0, 0, tiled=True)
    block = pl.pallas_call(
        sum_kernel,
        out_shape=jax.ShapeDtypeStruct((2 * n + 8, n), jnp.float32),
        in_specs=[VMEM],
        out_specs=VMEM,
        compiler_params=PARAMS,
    )(partial).astype(jnp.float16)

    a, b = [lax.ppermute(block, AXES, p).astype(jnp.float32) for p in perms]
    codes = table[:, 0::2] + 2 * table[:, 1::2]
    todo = jnp.asarray(codes[:, 0] + 8 * codes[:, 1])
    where = jnp.stack([lax.axis_index(a) for a in AXES])
    out = jax.ShapeDtypeStruct((n, 2 * n), jnp.float32)
    return pl.pallas_call(
        functools.partial(place_kernel, total_draws),
        out_shape=(out, out),
        in_specs=[SMEM, SMEM, VMEM, VMEM],
        out_specs=(VMEM, VMEM),
        compiler_params=PARAMS,
    )(where, todo, a, b)


def solution(mesh):
    grid = Mesh(mesh.devices.reshape(SIZES), AXES)
    return jax.shard_map(
        on_device,
        mesh=grid,
        in_specs=(P(("yh", "x", "c"), ("yl", "z")),) * 2,
        out_specs=(P(("yl", "z"), ("yh", "x", "c")),) * 2,
        check_vma=False,
    )
```

```python
import functools

import jax
import jax.numpy as jnp
import numpy as np
from jax import lax
from jax.experimental import pallas as pl
from jax.experimental.pallas import tpu as pltpu
from jax.sharding import Mesh, PartitionSpec as P

AXES = ("yh", "x", "c", "yl", "z")
SIZES = (2, 4, 2, 2, 16)
PIECES = 4
SCALES = [float(np.float32(2 ** (i / 8))) for i in range(8)]
TOP = 14.0
EXTRA = 16
VMEM = pl.BlockSpec(memory_space=pltpu.VMEM)
SMEM = pl.BlockSpec(memory_space=pltpu.SMEM)
PARAMS = pltpu.CompilerParams(vmem_limit_bytes=40 * 1024 * 1024)


def device_index(yh, x, c, yl, z):
    return (((yh * 4 + x) * 2 + c) * 2 + yl) * 16 + z


def home(row_y, row_z, col_y, col_z):
    return device_index(col_y, col_z // 4, col_z % 4 // 2, row_y, row_z), col_z % 2


def rank_or_slot(i, core, y):
    return i ^ (4 * (y ^ (1 - core)))


def homes(yh, x, c, yl, z):
    slot = rank_or_slot(yh * 4 + x, c, yl)
    if c == 0:
        left = (yl, z) if slot > 3 else (1 - yl, z + 4)
        right = (yl, z - slot % 4 - 1)
        if slot == 3 and yl == 1:
            right = (yl, z)
    else:
        left = (1 - yl, z) if slot > 3 else (yl, z - 4)
        right = (yl, z + slot % 4 + 1)
        if slot == 3 and (z < 8) != (yl == 0):
            return [home(0, z, 0, z) + (2,), home(1, z, 1, z) + (3,)]
        if slot == 7 and yl == 0:
            right = (yl, z)
    left, right = (left[0], left[1] % 16), (right[0], right[1] % 16)
    return [home(*left, *right) + (0,), home(*right, *left) + (1,)]


def routes():
    edges = []
    for place in np.ndindex(*SIZES):
        for to, half, mode in homes(*place):
            edges.append((device_index(*place), to, half, mode))
    into = [[] for _ in range(512)]
    for e, edge in enumerate(edges):
        into[edge[1]].append(e)
    def hops(e):
        there = np.unravel_index(edges[e][0], SIZES), np.unravel_index(edges[e][1], SIZES)
        (h0, x0, _, l0, z0), (h1, x1, _, l1, z1) = there
        return sum(
            min((p - q) % n, (q - p) % n)
            for p, q, n in ((x0, x1, 4), (2 * h0 + l0, 2 * h1 + l1, 4), (z0, z1, 16))
        )

    turn = [-1] * len(edges)
    for first in range(len(edges)):
        e, ways = first, ([], [])
        while turn[e] < 0:
            turn[e] = 0
            pair = into[edges[e][1]]
            other = pair[0] + pair[1] - e
            turn[other] = 1
            ways[0].append(e)
            ways[1].append(other)
            e = other ^ 1
        costs = [sum(map(hops, way)) for way in ways]
        if ways[0] and costs[1] < costs[0]:
            for e in ways[0]:
                turn[e] = 1
            for e in ways[1]:
                turn[e] = 0
    perms = [[], []]
    table = np.zeros((512, 4), np.int32)
    for e, (source, to, half, mode) in enumerate(edges):
        perms[turn[e]].append((source, to))
        table[to, 2 * half] = turn[e]
        table[to, 2 * half + 1] = mode
    return perms, table


def features_kernel(field, backward, both, f, b, done, sems, out_sems):
    rows = field.shape[0] // PIECES
    copies, leaving = [], []
    for piece in range(PIECES):
        part = pl.ds(piece * rows, rows)
        copies.append(
            [
                pltpu.make_async_copy(src.at[part], dst.at[part], sems.at[i, piece])
                for i, (src, dst) in enumerate(((field, f), (backward, b)))
            ]
        )
        for copy in copies[-1]:
            copy.start()
    for piece in range(PIECES):
        part = pl.ds(piece * rows, rows)
        for copy in copies[piece]:
            copy.wait()
        wide = jnp.tanh(f[part, :].astype(jnp.float32))
        gated = (1.0 - wide * wide) * b[part, :].astype(jnp.float32)
        done[0, part, :] = wide.astype(jnp.bfloat16)
        done[1, part, :] = gated.astype(jnp.bfloat16)
        for i in range(2):
            leave = pltpu.make_async_copy(
                done.at[i, part], both.at[i, part], out_sems.at[i, piece]
            )
            leave.start()
            leaving.append(leave)
    for leave in leaving:
        leave.wait()


def product(left, right):
    return lax.dot_general(
        left, right, (((0,), (0,)), ((), ())), preferred_element_type=jnp.float32
    )


def scale_of(place):
    scale = jnp.float32(SCALES[0])
    for i in range(1, len(SCALES)):
        scale = jnp.where(place[3] == i, SCALES[i], scale)
    return scale


def store(out, place, slot, kernel, total):
    n, scale = out.shape[-1], scale_of(place)
    for j in range(total.shape[1] // n):
        block = total[:, j * n : (j + 1) * n] * scale
        to = rank_or_slot(slot + j, place[0], place[1])
        out[to, kernel * n : (kernel + 1) * n] = block.astype(jnp.bfloat16)


def cases(place):
    core, y, z = place[0], place[1], place[2]
    return (core == 1) & ((z < 8) != (y == 0)), (core == 1) & (y == 0), (core == 0) & (y == 1)


def early_kernel(place, *refs):
    first, second, near, (out, left, steps) = refs[0:4], refs[4:8], refs[8:10], refs[10:]
    core, y, scale = place[0], place[1], scale_of(place)
    packed, same, _ = cases(place)
    n = out.shape[-1]
    rows = near[0].shape[1]
    for slot in range(8):
        out[slot, 2 * n : 2 * n + EXTRA] = jnp.zeros((EXTRA, n), jnp.bfloat16)
    for kernel in range(2):
        for i, chain in enumerate((first, second)):
            part = pl.ds(i * rows, rows)
            for j in range(3):
                steps[kernel, part, j * n : (j + 1) * n] = chain[j + 1][kernel]

        def own(kernel=kernel):
            return jnp.concatenate([first[0][kernel], second[0][kernel]], axis=0)

        def other(kernel=kernel):
            return jnp.concatenate([near[0][kernel], near[1][kernel]], axis=0)

        @pl.when(core == 0)
        def _():
            left[kernel] = own()

        @pl.when(core == 1)
        def _():
            left[kernel] = other()

        total = product(left[kernel], steps[kernel, :, 0 : 3 * n])
        store(out, place, 4, kernel, total)

        @pl.when(same)
        def _():
            store(out, place, 7, kernel, product(other(), own()))

        @pl.when(packed)
        def _():
            mine, yours = product(own(), own()), product(other(), other())
            high = jnp.where(y == 0, mine, yours)
            low = jnp.where(y == 0, yours, mine)
            row = lax.broadcasted_iota(jnp.int32, (n, n), 0)
            col = lax.broadcasted_iota(jnp.int32, (n, n), 1)
            store(out, place, 3, kernel, jnp.where(row <= col, high, low))
            diagonal = jnp.sum(jnp.where(row == col, low, 0.0), axis=0, keepdims=True)
            line = lax.broadcasted_iota(jnp.int32, (EXTRA, n), 0)
            to = rank_or_slot(3, core, y)
            extra = out[to, 2 * n : 2 * n + EXTRA].astype(jnp.float32)
            extra = jnp.where(line == kernel, diagonal * scale, extra)
            out[to, 2 * n : 2 * n + EXTRA] = extra.astype(jnp.bfloat16)


def middle_kernel(place, first, second, far, left, _, __, out, steps, total):
    _, same, turned = cases(place)
    n = out.shape[-1]
    rows = far.shape[1]
    for kernel in range(2):
        last = jnp.concatenate([first[kernel], second[kernel]], axis=0)

        @pl.when(jnp.logical_not(same))
        def _():
            store(out, place, 7, kernel, product(left[kernel], last))

        @pl.when(turned)
        def _():
            steps[kernel, :, 3 * n :] = left[kernel]

        @pl.when(jnp.logical_not(turned))
        def _():
            steps[kernel, :, 3 * n :] = last

        total[kernel] = product(far[kernel], steps[kernel, rows:])


def late_kernel(place, far, steps, part, _, out):
    packed, _, _ = cases(place)
    n = out.shape[-1]
    rows = far.shape[1]
    for kernel in range(2):
        total = part[kernel] + product(far[kernel], steps[kernel, 0:rows])
        store(out, place, 0, kernel, total[:, : 3 * n])

        @pl.when(jnp.logical_not(packed))
        def _():
            store(out, place, 3, kernel, total[:, 3 * n :])


def sum_kernel(parts, out):
    n = out.shape[-1]
    total = sum(
        parts[i].astype(jnp.float32) * (1 / scale) for i, scale in enumerate(SCALES)
    )
    line = lax.broadcasted_iota(jnp.int32, (8, n), 0)
    extra = total[2 * n : 2 * n + 8]
    for kernel in range(2):
        block = total[kernel * n : (kernel + 1) * n]
        diagonal = total[2 * n + kernel : 2 * n + kernel + 1]
        most = jnp.maximum(
            jnp.max(jnp.abs(block), axis=0, keepdims=True), jnp.abs(diagonal)
        )
        power = jnp.ceil(jnp.log2(jnp.maximum(most, 1e-30)))
        factor = jnp.exp2(TOP - power)
        out[kernel * n : (kernel + 1) * n] = block * factor
        extra = jnp.where(line == kernel, diagonal * factor, extra)
        extra = jnp.where(line == 2 + kernel, power, extra)
    out[2 * n :] = extra


def place_kernel(total_draws, place, todo, a, b, feature, gradient):
    n = feature.shape[0]
    row = lax.broadcasted_iota(jnp.int32, (n, n), 0)
    col = lax.broadcasted_iota(jnp.int32, (n, n), 1)
    code = todo[device_index(*[place[i] for i in range(5)])]
    for kernel, out in enumerate((feature, gradient)):
        block, line = pl.ds(kernel * n, n), pl.ds(2 * n + kernel, 1)
        power = pl.ds(2 * n + 2 + kernel, 1)
        for half in range(2):
            second, mode = code // 8**half % 2 == 1, code // 8**half // 2 % 4
            factor = jnp.exp2(jnp.where(second, b[power, :], a[power, :]) - TOP)
            got = jnp.where(second, b[block, :], a[block, :]) * factor
            extra = jnp.where(second, b[line, :], a[line, :]) * factor
            turned = got.T
            lower = row > col
            plain = (mode == 0) | ((mode == 2) & (row <= col)) | ((mode == 3) & lower)
            value = jnp.where(plain, got, turned)
            value = jnp.where((mode == 3) & (row == col), extra, value)
            out[:, half * n : (half + 1) * n] = value / total_draws


def on_device(field, backward):
    draws, n = field.shape
    total_draws = draws * 16
    both = pl.pallas_call(
        features_kernel,
        out_shape=jax.ShapeDtypeStruct((2, draws, n), jnp.bfloat16),
        in_specs=[pl.BlockSpec(memory_space=pltpu.HBM)] * 2,
        out_specs=pl.BlockSpec(memory_space=pltpu.HBM),
        scratch_shapes=[
            pltpu.VMEM((draws, n), jnp.bfloat16),
            pltpu.VMEM((draws, n), jnp.bfloat16),
            pltpu.VMEM((2, draws, n), jnp.bfloat16),
            pltpu.SemaphoreType.DMA((2, PIECES)),
            pltpu.SemaphoreType.DMA((2, PIECES)),
        ],
        compiler_params=pltpu.CompilerParams(vmem_limit_bytes=60 * 1024 * 1024),
    )(field, backward)

    step, first_step = [], []
    for c in range(2):
        for z in range(16):
            step.append((c * 16 + z, c * 16 + (z + 1 - 2 * c) % 16))
            first_step.append((c * 16 + z, (1 - c) * 16 + (z + 2 * c - 1) % 16))
    place = jnp.stack([lax.axis_index(a) for a in ("c", "yl", "z", ("yh", "x"))])
    shape = jax.ShapeDtypeStruct((8, 2 * n + EXTRA, n), jnp.bfloat16)
    left_shape = jax.ShapeDtypeStruct((2, 2 * draws, n), jnp.bfloat16)
    steps_shape = jax.ShapeDtypeStruct((2, 2 * draws, 4 * n), jnp.bfloat16)
    total_shape = jax.ShapeDtypeStruct((2, n, 4 * n), jnp.float32)

    def call(kernel, out_shape, *args, aliases={}, flops=1):
        return pl.pallas_call(
            kernel,
            out_shape=out_shape,
            in_specs=[SMEM] + [VMEM] * len(args),
            out_specs=jax.tree.map(lambda _: VMEM, out_shape),
            input_output_aliases=aliases,
            compiler_params=PARAMS,
            cost_estimate=pl.CostEstimate(
                flops=flops * 8 * n * n * draws,
                bytes_accessed=28 * n * draws,
                transcendentals=0,
            ),
        )(place, *args)

    chains = [
        lax.ppermute(both, ("c", "z"), step),
        lax.ppermute(both, ("c", "z"), first_step),
    ]
    walk = [[], []]
    other = lax.ppermute(both, "c", [(0, 1), (1, 0)])
    partners = (("c", "yl"), [(2, 3), (3, 2)])
    for j in range(4):
        if j:
            chains = [lax.ppermute(chain, ("c", "z"), step) for chain in chains]
        if j == 0:
            own, chains[1] = lax.optimization_barrier((both, chains[1]))
            near = [lax.ppermute(own, *partners)]
            other, chains[0] = lax.optimization_barrier((other, chains[0]))
        if j == 1:
            again, chains[1] = lax.optimization_barrier((other, chains[1]))
            near.append(lax.ppermute(again, *partners))
            near[0], chains[1] = lax.optimization_barrier((near[0], chains[1]))
        if j == 3:
            partial, left, steps = call(
                early_kernel,
                (shape, left_shape, steps_shape),
                *(both, *walk[0], other, *walk[1], *near),
                flops=4,
            )
            partial, chains[1] = lax.optimization_barrier((partial, chains[1]))
        for chain, blocks in zip(chains, walk):
            blocks.append(chain)
    cross = [(0, 2), (1, 3), (2, 1), (3, 0)]
    far = [lax.ppermute(chain, ("c", "yl"), cross) for chain in chains]

    partial, steps, total = call(
        middle_kernel,
        (shape, steps_shape, total_shape),
        *(*chains, far[0], left, partial, steps),
        aliases={5: 0, 6: 1},
        flops=3,
    )
    perms, table = routes()
    partial = call(late_kernel, shape, far[1], steps, total, partial, aliases={4: 0}, flops=2)
    partial = lax.all_to_all(partial, ("yh", "x"), 0, 0, tiled=True)
    block = pl.pallas_call(
        sum_kernel,
        out_shape=jax.ShapeDtypeStruct((2 * n + 8, n), jnp.float32),
        in_specs=[VMEM],
        out_specs=VMEM,
        compiler_params=PARAMS,
    )(partial).astype(jnp.float16)

    a, b = [lax.ppermute(block, AXES, p).astype(jnp.float32) for p in perms]
    codes = table[:, 0::2] + 2 * table[:, 1::2]
    todo = jnp.asarray(codes[:, 0] + 8 * codes[:, 1])
    where = jnp.stack([lax.axis_index(a) for a in AXES])
    out = jax.ShapeDtypeStruct((n, 2 * n), jnp.float32)
    return pl.pallas_call(
        functools.partial(place_kernel, total_draws),
        out_shape=(out, out),
        in_specs=[SMEM, SMEM, VMEM, VMEM],
        out_specs=(VMEM, VMEM),
        compiler_params=PARAMS,
    )(where, todo, a, b)


def solution(mesh):
    grid = Mesh(mesh.devices.reshape(SIZES), AXES)
    return jax.shard_map(
        on_device,
        mesh=grid,
        in_specs=(P(("yh", "x", "c"), ("yl", "z")),) * 2,
        out_specs=(P(("yl", "z"), ("yh", "x", "c")),) * 2,
        check_vma=False,
    )
```

```python
import functools

import jax
import jax.numpy as jnp
import numpy as np
from jax import lax
from jax.experimental import pallas as pl
from jax.experimental.pallas import tpu as pltpu
from jax.sharding import Mesh, PartitionSpec as P

AXES = ("yh", "x", "c", "yl", "z")
SIZES = (2, 4, 2, 2, 16)
PIECES = 2
SCALES = [float(np.float32(2 ** (i / 8))) for i in range(8)]
TOP = 14.0
EXTRA = 16
VMEM = pl.BlockSpec(memory_space=pltpu.VMEM)
SMEM = pl.BlockSpec(memory_space=pltpu.SMEM)
PARAMS = pltpu.CompilerParams(vmem_limit_bytes=40 * 1024 * 1024)


def device_index(yh, x, c, yl, z):
    return (((yh * 4 + x) * 2 + c) * 2 + yl) * 16 + z


def home(row_y, row_z, col_y, col_z):
    return device_index(col_y, col_z // 4, col_z % 4 // 2, row_y, row_z), col_z % 2


def rank_or_slot(i, core, y):
    return i ^ (4 * (y ^ (1 - core)))


def homes(yh, x, c, yl, z):
    slot = rank_or_slot(yh * 4 + x, c, yl)
    if c == 0:
        left = (yl, z) if slot > 3 else (1 - yl, z + 4)
        right = (yl, z - slot % 4 - 1)
        if slot == 3 and yl == 1:
            right = (yl, z)
    else:
        left = (1 - yl, z) if slot > 3 else (yl, z - 4)
        right = (yl, z + slot % 4 + 1)
        if slot == 3 and (z < 8) != (yl == 0):
            return [home(0, z, 0, z) + (2,), home(1, z, 1, z) + (3,)]
        if slot == 7 and yl == 0:
            right = (yl, z)
    left, right = (left[0], left[1] % 16), (right[0], right[1] % 16)
    return [home(*left, *right) + (0,), home(*right, *left) + (1,)]


def routes():
    edges = []
    for place in np.ndindex(*SIZES):
        for to, half, mode in homes(*place):
            edges.append((device_index(*place), to, half, mode))
    into = [[] for _ in range(512)]
    for e, edge in enumerate(edges):
        into[edge[1]].append(e)
    def hops(e):
        there = np.unravel_index(edges[e][0], SIZES), np.unravel_index(edges[e][1], SIZES)
        (h0, x0, _, l0, z0), (h1, x1, _, l1, z1) = there
        return sum(
            w * min((p - q) % n, (q - p) % n)
            for p, q, n, w in ((x0, x1, 4, 1), (2 * h0 + l0, 2 * h1 + l1, 4, 1), (z0, z1, 16, 2))
        )

    turn = [-1] * len(edges)
    for first in range(len(edges)):
        e, ways = first, ([], [])
        while turn[e] < 0:
            turn[e] = 0
            pair = into[edges[e][1]]
            other = pair[0] + pair[1] - e
            turn[other] = 1
            ways[0].append(e)
            ways[1].append(other)
            e = other ^ 1
        costs = [sum(map(hops, way)) for way in ways]
        if ways[0] and costs[1] < costs[0]:
            for e in ways[0]:
                turn[e] = 1
            for e in ways[1]:
                turn[e] = 0
    perms = [[], []]
    table = np.zeros((512, 4), np.int32)
    for e, (source, to, half, mode) in enumerate(edges):
        perms[turn[e]].append((source, to))
        table[to, 2 * half] = turn[e]
        table[to, 2 * half + 1] = mode
    return perms, table


def features_kernel(field, backward, both, f, b, sems):
    rows = field.shape[0] // PIECES
    copies = []
    for piece in range(PIECES):
        part = pl.ds(piece * rows, rows)
        copies.append(
            [
                pltpu.make_async_copy(src.at[part], dst.at[part], sems.at[i, piece])
                for i, (src, dst) in enumerate(((field, f), (backward, b)))
            ]
        )
        for copy in copies[-1]:
            copy.start()
    for piece in range(PIECES):
        part = pl.ds(piece * rows, rows)
        for copy in copies[piece]:
            copy.wait()
        wide = jnp.tanh(f[part, :].astype(jnp.float32))
        gated = (1.0 - wide * wide) * b[part, :].astype(jnp.float32)
        both[0, part, :] = wide.astype(jnp.bfloat16)
        both[1, part, :] = gated.astype(jnp.bfloat16)


def product(left, right):
    return lax.dot_general(
        left, right, (((0,), (0,)), ((), ())), preferred_element_type=jnp.float32
    )


def scale_of(place):
    scale = jnp.float32(SCALES[0])
    for i in range(1, len(SCALES)):
        scale = jnp.where(place[3] == i, SCALES[i], scale)
    return scale


def store(out, place, slot, kernel, total):
    n, scale = out.shape[-1], scale_of(place)
    for j in range(total.shape[1] // n):
        block = total[:, j * n : (j + 1) * n] * scale
        to = rank_or_slot(slot + j, place[0], place[1])
        out[to, kernel * n : (kernel + 1) * n] = block.astype(jnp.bfloat16)


def cases(place):
    core, y, z = place[0], place[1], place[2]
    return (core == 1) & ((z < 8) != (y == 0)), (core == 1) & (y == 0), (core == 0) & (y == 1)


def early_kernel(place, *refs):
    first, second, near, (out, left, steps) = refs[0:4], refs[4:8], refs[8:10], refs[10:]
    core, y, scale = place[0], place[1], scale_of(place)
    packed, same, _ = cases(place)
    n = out.shape[-1]
    rows = near[0].shape[1]
    for slot in range(8):
        out[slot, 2 * n : 2 * n + EXTRA] = jnp.zeros((EXTRA, n), jnp.bfloat16)
    for kernel in range(2):
        for i, chain in enumerate((first, second)):
            part = pl.ds(i * rows, rows)
            for j in range(3):
                steps[kernel, part, j * n : (j + 1) * n] = chain[j + 1][kernel]

        def own(kernel=kernel):
            return jnp.concatenate([first[0][kernel], second[0][kernel]], axis=0)

        def other(kernel=kernel):
            return jnp.concatenate([near[0][kernel], near[1][kernel]], axis=0)

        @pl.when(core == 0)
        def _():
            left[kernel] = own()

        @pl.when(core == 1)
        def _():
            left[kernel] = other()

        total = product(left[kernel], steps[kernel, :, 0 : 3 * n])
        store(out, place, 4, kernel, total)

        @pl.when(same)
        def _():
            store(out, place, 7, kernel, product(other(), own()))

        @pl.when(packed)
        def _():
            mine, yours = product(own(), own()), product(other(), other())
            high = jnp.where(y == 0, mine, yours)
            low = jnp.where(y == 0, yours, mine)
            row = lax.broadcasted_iota(jnp.int32, (n, n), 0)
            col = lax.broadcasted_iota(jnp.int32, (n, n), 1)
            store(out, place, 3, kernel, jnp.where(row <= col, high, low))
            diagonal = jnp.sum(jnp.where(row == col, low, 0.0), axis=0, keepdims=True)
            line = lax.broadcasted_iota(jnp.int32, (EXTRA, n), 0)
            to = rank_or_slot(3, core, y)
            extra = out[to, 2 * n : 2 * n + EXTRA].astype(jnp.float32)
            extra = jnp.where(line == kernel, diagonal * scale, extra)
            out[to, 2 * n : 2 * n + EXTRA] = extra.astype(jnp.bfloat16)


def middle_kernel(place, first, second, far, left, _, __, out, steps, total):
    _, same, turned = cases(place)
    n = out.shape[-1]
    rows = far.shape[1]
    for kernel in range(2):
        last = jnp.concatenate([first[kernel], second[kernel]], axis=0)

        @pl.when(jnp.logical_not(same))
        def _():
            store(out, place, 7, kernel, product(left[kernel], last))

        @pl.when(turned)
        def _():
            steps[kernel, :, 3 * n :] = left[kernel]

        @pl.when(jnp.logical_not(turned))
        def _():
            steps[kernel, :, 3 * n :] = last

        total[kernel] = product(far[kernel], steps[kernel, rows:])


def late_kernel(place, far, steps, part, _, out):
    packed, _, _ = cases(place)
    n = out.shape[-1]
    rows = far.shape[1]
    for kernel in range(2):
        total = part[kernel] + product(far[kernel], steps[kernel, 0:rows])
        store(out, place, 0, kernel, total[:, : 3 * n])

        @pl.when(jnp.logical_not(packed))
        def _():
            store(out, place, 3, kernel, total[:, 3 * n :])


def sum_kernel(parts, out):
    n = out.shape[-1]
    total = sum(
        parts[i].astype(jnp.float32) * (1 / scale) for i, scale in enumerate(SCALES)
    )
    line = lax.broadcasted_iota(jnp.int32, (8, n), 0)
    extra = total[2 * n : 2 * n + 8]
    for kernel in range(2):
        block = total[kernel * n : (kernel + 1) * n]
        diagonal = total[2 * n + kernel : 2 * n + kernel + 1]
        most = jnp.maximum(
            jnp.max(jnp.abs(block), axis=0, keepdims=True), jnp.abs(diagonal)
        )
        power = jnp.ceil(jnp.log2(jnp.maximum(most, 1e-30)))
        factor = jnp.exp2(TOP - power)
        out[kernel * n : (kernel + 1) * n] = block * factor
        extra = jnp.where(line == kernel, diagonal * factor, extra)
        extra = jnp.where(line == 2 + kernel, power, extra)
    out[2 * n :] = extra


def place_kernel(total_draws, place, todo, a, b, feature, gradient):
    n = feature.shape[0]
    row = lax.broadcasted_iota(jnp.int32, (n, n), 0)
    col = lax.broadcasted_iota(jnp.int32, (n, n), 1)
    code = todo[device_index(*[place[i] for i in range(5)])]
    for kernel, out in enumerate((feature, gradient)):
        block, line = pl.ds(kernel * n, n), pl.ds(2 * n + kernel, 1)
        power = pl.ds(2 * n + 2 + kernel, 1)
        for half in range(2):
            second, mode = code // 8**half % 2 == 1, code // 8**half // 2 % 4
            factor = jnp.exp2(jnp.where(second, b[power, :], a[power, :]) - TOP)
            got = jnp.where(second, b[block, :], a[block, :]) * factor
            extra = jnp.where(second, b[line, :], a[line, :]) * factor
            turned = got.T
            lower = row > col
            plain = (mode == 0) | ((mode == 2) & (row <= col)) | ((mode == 3) & lower)
            value = jnp.where(plain, got, turned)
            value = jnp.where((mode == 3) & (row == col), extra, value)
            out[:, half * n : (half + 1) * n] = value / total_draws


def on_device(field, backward):
    draws, n = field.shape
    total_draws = draws * 16
    both = pl.pallas_call(
        features_kernel,
        out_shape=jax.ShapeDtypeStruct((2, draws, n), jnp.bfloat16),
        in_specs=[pl.BlockSpec(memory_space=pltpu.HBM)] * 2,
        out_specs=VMEM,
        scratch_shapes=[
            pltpu.VMEM((draws, n), jnp.bfloat16),
            pltpu.VMEM((draws, n), jnp.bfloat16),
            pltpu.SemaphoreType.DMA((2, PIECES)),
        ],
        compiler_params=pltpu.CompilerParams(vmem_limit_bytes=60 * 1024 * 1024),
    )(field, backward)

    step, first_step = [], []
    for c in range(2):
        for z in range(16):
            step.append((c * 16 + z, c * 16 + (z + 1 - 2 * c) % 16))
            first_step.append((c * 16 + z, (1 - c) * 16 + (z + 2 * c - 1) % 16))
    place = jnp.stack([lax.axis_index(a) for a in ("c", "yl", "z", ("yh", "x"))])
    shape = jax.ShapeDtypeStruct((8, 2 * n + EXTRA, n), jnp.bfloat16)
    left_shape = jax.ShapeDtypeStruct((2, 2 * draws, n), jnp.bfloat16)
    steps_shape = jax.ShapeDtypeStruct((2, 2 * draws, 4 * n), jnp.bfloat16)
    total_shape = jax.ShapeDtypeStruct((2, n, 4 * n), jnp.float32)

    def call(kernel, out_shape, *args, aliases={}, flops=1):
        return pl.pallas_call(
            kernel,
            out_shape=out_shape,
            in_specs=[SMEM] + [VMEM] * len(args),
            out_specs=jax.tree.map(lambda _: VMEM, out_shape),
            input_output_aliases=aliases,
            compiler_params=PARAMS,
            cost_estimate=pl.CostEstimate(
                flops=flops * 8 * n * n * draws,
                bytes_accessed=28 * n * draws,
                transcendentals=0,
            ),
        )(place, *args)

    chains = [
        lax.ppermute(both, ("c", "z"), step),
        lax.ppermute(both, ("c", "z"), first_step),
    ]
    walk = [[], []]
    other = lax.ppermute(both, "c", [(0, 1), (1, 0)])
    partners = (("c", "yl"), [(2, 3), (3, 2)])
    for j in range(4):
        if j:
            chains = [lax.ppermute(chain, ("c", "z"), step) for chain in chains]
        if j == 0:
            own, chains[1] = lax.optimization_barrier((both, chains[1]))
            near = [lax.ppermute(own, *partners)]
            other, chains[0] = lax.optimization_barrier((other, chains[0]))
        if j == 1:
            again, chains[1] = lax.optimization_barrier((other, chains[1]))
            near.append(lax.ppermute(again, *partners))
            near[0], chains[1] = lax.optimization_barrier((near[0], chains[1]))
        if j == 3:
            partial, left, steps = call(
                early_kernel,
                (shape, left_shape, steps_shape),
                *(both, *walk[0], other, *walk[1], *near),
                flops=4,
            )
            partial, chains[1] = lax.optimization_barrier((partial, chains[1]))
        for chain, blocks in zip(chains, walk):
            blocks.append(chain)
    cross = [(0, 2), (1, 3), (2, 1), (3, 0)]
    far = [lax.ppermute(chain, ("c", "yl"), cross) for chain in chains]

    partial, steps, total = call(
        middle_kernel,
        (shape, steps_shape, total_shape),
        *(*chains, far[0], left, partial, steps),
        aliases={5: 0, 6: 1},
        flops=3,
    )
    perms, table = routes()
    partial = call(late_kernel, shape, far[1], steps, total, partial, aliases={4: 0}, flops=2)
    partial = lax.all_to_all(partial, ("yh", "x"), 0, 0, tiled=True)
    block = pl.pallas_call(
        sum_kernel,
        out_shape=jax.ShapeDtypeStruct((2 * n + 8, n), jnp.float32),
        in_specs=[VMEM],
        out_specs=VMEM,
        compiler_params=PARAMS,
    )(partial).astype(jnp.float16)

    a, b = [lax.ppermute(block, AXES, p).astype(jnp.float32) for p in perms]
    codes = table[:, 0::2] + 2 * table[:, 1::2]
    todo = jnp.asarray(codes[:, 0] + 8 * codes[:, 1])
    where = jnp.stack([lax.axis_index(a) for a in AXES])
    out = jax.ShapeDtypeStruct((n, 2 * n), jnp.float32)
    return pl.pallas_call(
        functools.partial(place_kernel, total_draws),
        out_shape=(out, out),
        in_specs=[SMEM, SMEM, VMEM, VMEM],
        out_specs=(VMEM, VMEM),
        compiler_params=PARAMS,
    )(where, todo, a, b)


def solution(mesh):
    grid = Mesh(mesh.devices.reshape(SIZES), AXES)
    return jax.shard_map(
        on_device,
        mesh=grid,
        in_specs=(P(("yh", "x", "c"), ("yl", "z")),) * 2,
        out_specs=(P(("yl", "z"), ("yh", "x", "c")),) * 2,
        check_vma=False,
    )
```
